512 devices in a mesh: dp: 64 (over z, x, core), tensor: 8 (over y).
Axes of the slice: x: 4, y: 8, z: 8, core: 2. Of those that a mesh axis runs over, the one named last changes fastest.
Arguments:
- gradients: bfloat16 [8, 512, 256, 256], P(None, 'tensor', 'dp')
- owners: int32 [512], P('tensor'), may hold values from 0 to 63, as said below
- left_stats: float32 [1024, 256, 256], P(('dp', 'tensor')), as said below
- right_stats: float32 [1024, 256, 256], P(('dp', 'tensor')), as said below
- left_roots: bfloat16 [1024, 256, 256], P(('dp', 'tensor')), as said below
- right_roots: bfloat16 [1024, 256, 256], P(('dp', 'tensor')), as said below
Outputs:
- preconditioned: bfloat16 [8, 512, 256, 256], P(None, 'tensor', 'dp')
- left_updated: float32 [1024, 256, 256], P(('dp', 'tensor'))
- right_updated: float32 [1024, 256, 256], P(('dp', 'tensor'))
The draws below stay inside these ranges and needn't reach their ends.
Inputs may be any that keep to these rules, and one draw needn't show every extreme that they name: Each tensor shard's 64 blocks name dp indices as owners; no index is named by more than 2 blocks of one shard, and in every shard some index is named by exactly 2. `left_stats`: every slot's matrix is symmetric. `right_stats`: every slot's matrix is symmetric. `left_roots`: every slot's matrix is symmetric. `right_roots`: every slot's matrix is symmetric.
All inputs are finite; a program needn't handle non-finite values.
Results may differ from the reference program's by a relative error of at most 0.0049.
Values may be sent and summed in bfloat16 or wider, within the bound.
A program may use at most 64 MiB of HBM per device.

```python
import math
import jax
import jax.numpy as jnp
from jax import lax

BLOCK = 256
SLOTS = 2
STEPS = 8
SHARD_BLOCKS = 64
BLOCKS = 512
SLOTS_ALL = 1024


def symmetric_matrices(key, matrix_count, lowest, highest, spread):
    key_diagonal, key_outside = jax.random.split(key)
    diagonal = jnp.exp(jax.random.uniform(key_diagonal, (matrix_count, BLOCK), minval=math.log(lowest), maxval=math.log(highest)))
    raw_outside = jax.random.uniform(key_outside, (matrix_count, BLOCK, BLOCK), minval=-spread, maxval=spread)
    outside = raw_outside + jnp.swapaxes(raw_outside, 1, 2)
    identity = jnp.eye(BLOCK, dtype=jnp.float32)
    return outside * (1.0 - identity) + diagonal[:, :, None] * identity


def draw_left_stats(key, part):
    key = jax.random.fold_in(key, 11)
    return symmetric_matrices(key, SLOTS_ALL, 0.6, 2.0, 0.021)


def draw_right_stats(key, part):
    key = jax.random.fold_in(key, 13)
    return symmetric_matrices(key, SLOTS_ALL, 0.6, 2.0, 0.021)


def draw_left_roots(key, part):
    key = jax.random.fold_in(key, 17)
    return symmetric_matrices(key, SLOTS_ALL, 1.0, 3.0, 0.03).astype(jnp.bfloat16)


def draw_right_roots(key, part):
    key = jax.random.fold_in(key, 19)
    return symmetric_matrices(key, SLOTS_ALL, 1.0, 3.0, 0.03).astype(jnp.bfloat16)


def draw_gradients(key, part):
    key = jax.random.fold_in(key, 3)
    keys = jax.random.split(key, 6)
    shard_count = BLOCKS // SHARD_BLOCKS
    rows = jnp.arange(BLOCK, dtype=jnp.float32) / (BLOCK - 1)
    shard_place = (jnp.arange(BLOCKS) // SHARD_BLOCKS).astype(jnp.float32) / max(shard_count - 1, 1)
    row_scale = (1.0 + 2.0 * rows) * jnp.exp(0.5 * math.log(10.0) * jax.random.uniform(keys[0], (BLOCK,)))
    column_scale = jnp.exp(0.5 * math.log(10.0) * jax.random.uniform(keys[1], (BLOCK,)))
    block_scale = (1.0 + 2.0 * shard_place) * jnp.exp(math.log(2.0) * jax.random.uniform(keys[2], (BLOCKS,)))
    step_order = jax.random.permutation(keys[5], STEPS)
    step_scale = jnp.where(step_order < STEPS // 2, 0.004, 1.0).astype(jnp.float32)
    noise = jax.random.normal(keys[3], (STEPS, BLOCKS, BLOCK, BLOCK))
    return (2.0 * noise * step_scale[:, None, None, None] * block_scale[None, :, None, None] * row_scale[None, None, :, None] * column_scale[None, None, None, :]).astype(jnp.bfloat16)


def shard_owners(key):
    first_key, second_key, third_key = jax.random.split(key, 3)
    owner_count = SHARD_BLOCKS
    quarter = owner_count // 4
    doubled = jax.random.randint(third_key, (), 1, quarter + 1)
    order = jax.random.permutation(first_key, owner_count)
    rank = jnp.argsort(order).astype(jnp.int32)
    load = 1 + (rank < doubled).astype(jnp.int32) - ((rank >= doubled) & (rank < 2 * doubled)).astype(jnp.int32)
    ends = jnp.cumsum(load)
    position = jnp.arange(SHARD_BLOCKS, dtype=jnp.int32)
    listing = jnp.sum((ends[None, :] <= position[:, None]).astype(jnp.int32), axis=1)
    mixing = jax.random.permutation(second_key, SHARD_BLOCKS)
    return listing[mixing].astype(jnp.int32)


def draw_owners(key, part):
    key = jax.random.fold_in(key, 7)
    shard_count = BLOCKS // SHARD_BLOCKS
    keys = jax.random.split(key, shard_count)
    return jax.vmap(shard_owners)(keys).reshape(-1).astype(jnp.int32)


def setup_inputs(seed: int = 0) -> dict:
    key_list = jax.random.split(jax.random.key(seed), 7)
    gradients = draw_gradients(jax.random.fold_in(key_list[6], 71), 0)
    owners = draw_owners(jax.random.fold_in(key_list[6], 71), 0)
    left_stats = draw_left_stats(jax.random.fold_in(key_list[6], 71), 0)
    right_stats = draw_right_stats(jax.random.fold_in(key_list[6], 71), 0)
    left_roots = draw_left_roots(jax.random.fold_in(key_list[6], 71), 0)
    right_roots = draw_right_roots(jax.random.fold_in(key_list[6], 71), 0)
    return {"gradients": gradients, "owners": owners, "left_stats": left_stats, "right_stats": right_stats, "left_roots": left_roots, "right_roots": right_roots}


SECOND_MOMENT = 0.95
CLIP_EPSILON = 1e-06
GRAFT_EPSILON = 1e-06

def slot_numbers(owner_row):
    block_count = owner_row.shape[0]
    position = jnp.arange(block_count, dtype=jnp.int32)
    same_owner = owner_row[:, None] == owner_row[None, :]
    earlier = position[None, :] < position[:, None]
    return lax.optimization_barrier(jnp.sum((same_owner & earlier).astype(jnp.int32), axis=1)).astype(jnp.int32)

def reference(gradients, owners, left_stats, right_stats, left_roots, right_roots):
    shard_count = BLOCKS // SHARD_BLOCKS

    def step_square(moment_gradients):
        return jnp.sum(jnp.square(moment_gradients.astype(jnp.float32)))
    totals = lax.map(step_square, gradients)
    clip_factor = jnp.minimum(1.0, 1.0 / jnp.sqrt(totals / (BLOCKS * BLOCK * BLOCK) + CLIP_EPSILON))
    owner_rows = owners.reshape(shard_count, SHARD_BLOCKS)
    slot_index = jax.vmap(slot_numbers)(owner_rows)
    shard_index = jnp.arange(shard_count, dtype=jnp.int32)[:, None]
    state_index = ((owner_rows * shard_count + shard_index) * SLOTS + slot_index).reshape(-1).astype(jnp.int32)

    def one_block(position):
        target_slot = state_index[position]
        moments = lax.dynamic_index_in_dim(gradients, position, 1, keepdims=False)
        left_gram = left_stats[target_slot]
        right_gram = right_stats[target_slot]
        left_root = left_roots[target_slot]
        right_root = right_roots[target_slot]
        results = []
        for moment in range(STEPS):
            gradient = moments[moment]
            gradient_wide = gradient.astype(jnp.float32)
            weight = (1.0 - SECOND_MOMENT) * clip_factor[moment] * clip_factor[moment] / BLOCK
            left_gram = SECOND_MOMENT * left_gram + weight * jnp.dot(gradient, gradient.T, preferred_element_type=jnp.float32)
            right_gram = SECOND_MOMENT * right_gram + weight * jnp.dot(gradient.T, gradient, preferred_element_type=jnp.float32)
            left_part = jnp.dot(left_root, gradient, preferred_element_type=jnp.float32).astype(jnp.bfloat16)
            direction = jnp.dot(left_part, right_root, preferred_element_type=jnp.float32)
            graft_ratio = clip_factor[moment] * jnp.sqrt(jnp.mean(gradient_wide * gradient_wide)) / jnp.sqrt(jnp.mean(direction * direction) + GRAFT_EPSILON)
            results.append((graft_ratio * direction).astype(jnp.bfloat16))
        return (jnp.stack(results), left_gram, right_gram)
    updates, left_all, right_all = lax.map(one_block, jnp.arange(BLOCKS, dtype=jnp.int32))
    preconditioned = jnp.transpose(updates, (1, 0, 2, 3))
    left_updated = left_stats.at[state_index].set(left_all)
    right_updated = right_stats.at[state_index].set(right_all)
    return (preconditioned, left_updated, right_updated)
```

```python
import functools

import jax
import jax.numpy as jnp
from jax import lax
from jax.experimental import pallas as pl
from jax.experimental.pallas import tpu as pltpu
from jax.sharding import PartitionSpec as P

SECOND_MOMENT = 0.95
CLIP_EPSILON = 1e-06
GRAFT_EPSILON = 1e-06
MESH = pl.DeviceIdType.MESH

CHUNKS = 2
TILE_ROWS, TILE_COLS = 16, 128


def routes(owners):
    count = owners.shape[0]
    position = jnp.arange(count, dtype=jnp.int32)
    same_owner = owners[:, None] == owners[None, :]
    earlier = position[None, :] < position[:, None]
    slot = jnp.sum((same_owner & earlier).astype(jnp.int32), axis=1)
    owned = owners[None, :] == position[:, None]
    first = owned & (slot == 0)[None, :]
    second = owned & (slot == 1)[None, :]
    has_first = jnp.any(first, axis=1)
    has_second = jnp.any(second, axis=1)
    first_block = jnp.sum(jnp.where(first, position[None, :], 0), axis=1)
    second_block = jnp.sum(jnp.where(second, position[None, :], 0), axis=1)
    before = position[None, :] < position[:, None]
    empty_rank = jnp.sum((before & ~has_first[None, :]).astype(jnp.int32), axis=1)
    second_rank = jnp.sum((before & has_second[None, :]).astype(jnp.int32), axis=1)
    match = (
        (empty_rank[:, None] == second_rank[None, :])
        & ~has_first[:, None]
        & has_second[None, :]
    )
    helped = jnp.sum(jnp.where(match, position[None, :], 0), axis=1)
    helper = jnp.sum(jnp.where(match, position[:, None], 0), axis=0)
    helped_block = jnp.sum(jnp.where(match, second_block[None, :], 0), axis=1)
    block_of = jnp.where(has_first, first_block, helped_block)
    device_of = jnp.sum(
        jnp.where(block_of[:, None] == position[None, :], position[:, None], 0), axis=0
    )
    return jnp.stack(
        [
            block_of,
            device_of,
            helped,
            helper,
            has_first.astype(jnp.int32),
            has_second.astype(jnp.int32),
        ]
    )


def kernel(
    sizes,
    table,
    x_ref,
    left_stats,
    right_stats,
    left_roots,
    right_roots,
    y_ref,
    left_out,
    right_out,
    byblock,
    stage,
    land,
    grads,
    outs,
    back_stage,
    back_first,
    back_second,
    roots_a,
    roots_b,
    roots_c,
    roots_d,
    grams_a,
    grams_b,
    grams_c,
    grams_d,
    root_use,
    gram_sum,
    sums_y,
    sums_dp,
    send_y,
    recv_y,
    send_dp,
    recv_dp,
    send_tile,
    recv_tile,
    send_go,
    recv_go,
    send_back,
    recv_back,
):
    steps, holders, shards, piece, width, total_count = sizes
    back = (back_first, back_second)
    chunk_steps = steps // CHUNKS
    rows = piece * chunk_steps
    group = width // rows
    groups = holders // group
    span = group * piece
    me = lax.axis_index("dp")
    shard = lax.axis_index("tensor")

    def peer(k):
        return lax.rem(me + k, holders)

    barrier = pltpu.get_barrier_semaphore()

    def greet(k, carry):
        pl.semaphore_signal(barrier, inc=1, device_id=(peer(k), shard), device_id_type=MESH)
        return carry

    def greet_shard(k, carry):
        pl.semaphore_signal(
            barrier, inc=1, device_id=(me, lax.rem(shard + k, shards)), device_id_type=MESH
        )
        return carry

    lax.fori_loop(1, shards, greet_shard, 0)
    lax.fori_loop(1, holders, greet, 0)

    lane = lax.broadcasted_iota(jnp.int32, (1, TILE_COLS), 1)

    def add_square(s, row):
        values = x_ref[s].astype(jnp.float32)
        square = jnp.sum(values * values, axis=(0, 1), keepdims=True)
        return row + jnp.where(lane == s, square, 0.0)

    local_row = lax.fori_loop(0, steps, add_square, jnp.zeros((1, TILE_COLS), jnp.float32))
    sums_y[pl.ds(shard, 1)] = local_row[None]

    out_index = lax.broadcasted_iota(jnp.int32, (width, width), 0)
    in_index = lax.broadcasted_iota(jnp.int32, (width, width), 1)

    def by_device(index):
        step, rest = index // span, index % span
        return (rest // piece) * rows + step * piece + rest % piece

    apart = (out_index == by_device(in_index)).astype(jnp.bfloat16)
    together = (by_device(out_index) == in_index).astype(jnp.bfloat16)

    def permute(matrix, values):
        return jnp.dot(matrix, values, preferred_element_type=jnp.float32).astype(jnp.bfloat16)

    def split_by_device(c, g, source, target):
        part = source[pl.ds(c * chunk_steps, chunk_steps), pl.ds(g * span, span), :]
        done = permute(apart, part.reshape(width, width))
        target[c, pl.ds(g * group, group)] = done.reshape(group, rows, width)

    def prepare(i, carry):
        split_by_device(i // groups, i % groups, x_ref, byblock)
        return carry

    lax.fori_loop(0, CHUNKS * groups, prepare, 0)

    row_tiles, col_tiles = width // TILE_ROWS, width // TILE_COLS

    def tiles_of(matrix, target, base):
        for i in range(row_tiles):
            for j in range(col_tiles):
                target[base + i * col_tiles + j] = matrix[
                    i * TILE_ROWS : (i + 1) * TILE_ROWS, j * TILE_COLS : (j + 1) * TILE_COLS
                ]

    def matrix_of(source, base):
        return jnp.concatenate(
            [
                jnp.concatenate([source[base + i * col_tiles + j] for j in range(col_tiles)], axis=1)
                for i in range(row_tiles)
            ],
            axis=0,
        )

    half = row_tiles * col_tiles
    tiles_of(left_roots[1], roots_a, 0)
    tiles_of(right_roots[1], roots_a, half)

    pl.semaphore_wait(barrier, holders - 1 + shards - 1)

    def copy(source, target, send, recv, device, t=None):
        return pltpu.make_async_remote_copy(
            src_ref=source,
            dst_ref=target,
            send_sem=send,
            recv_sem=recv,
            device_id=(device, shard if t is None else t),
            device_id_type=MESH,
        )

    def wait_bytes(ref, count, semaphore):
        part = ref.at[pl.ds(0, count)]
        pltpu.make_async_copy(part, part, semaphore).wait()

    def send_shard(k, carry):
        t = lax.rem(shard + k, shards)
        copy(sums_y.at[shard], sums_y.at[shard], send_y, recv_y, me, t).start()
        return carry

    lax.fori_loop(1, shards, send_shard, 0)

    def send_tiles(source, target, which):
        def one(k, carry):
            d = peer(k)
            copy(
                source.at[d], target.at[me], send_tile.at[which], recv_tile.at[which], d
            ).start()
            return carry

        lax.fori_loop(1, holders, one, 0)
        target[pl.ds(me, 1)] = source[pl.ds(me, 1)]

    def pass_tiles(source, staged, target, which, row):
        def one(k, carry):
            d = peer(k)
            staged[d] = source[table[row, d]]
            copy(
                staged.at[d], target.at[me], send_tile.at[which], recv_tile.at[which], d
            ).start()
            return carry

        lax.fori_loop(1, holders, one, 0)
        target[me] = source[table[row, me]]

    send_tiles(roots_a, roots_b, 0)

    def send_gradients(c):
        def one(k, carry):
            d = peer(k)
            stage[c, d] = byblock[c, table[0, d]]
            copy(stage.at[c, d], land.at[c, me], send_go.at[c], recv_go.at[c], d).start()
            return carry

        lax.fori_loop(1, holders, one, 0)
        land[c, me] = byblock[c, table[0, me]]

    send_gradients(0)

    wait_bytes(sums_y, shards - 1, recv_y)
    shard_row = sums_y[0]
    for t in range(1, shards):
        shard_row = shard_row + sums_y[t]
    sums_dp[pl.ds(me, 1)] = shard_row[None]

    def send_sums(k, carry):
        d = peer(k)
        copy(sums_dp.at[me], sums_dp.at[me], send_dp, recv_dp, d).start()
        return carry

    lax.fori_loop(1, holders, send_sums, 0)

    wait_bytes(roots_b, holders - 1, recv_tile.at[0])
    pass_tiles(roots_b, roots_c, roots_d, 1, 2)

    for c in range(1, CHUNKS):
        send_gradients(c)

    wait_bytes(sums_dp, holders - 1, recv_dp)
    totals = jnp.sum(sums_dp[...], axis=0)
    clip_row = jnp.minimum(1.0, 1.0 / jnp.sqrt(totals / total_count + CLIP_EPSILON))

    def clip_of(s):
        return jnp.sum(jnp.where(lane == s, clip_row, 0.0), axis=1, keepdims=True)

    has_first = table[4, me]
    has_second = table[5, me]

    def gather_steps(c):
        wait_bytes(land.at[c], holders - 1, recv_go.at[c])

        def one(g, carry):
            values = land[c, pl.ds(g * group, group)].reshape(width, width)
            done = permute(together, values).reshape(chunk_steps, span, width)
            grads[pl.ds(c * chunk_steps, chunk_steps), pl.ds(g * span, span), :] = done
            return carry

        lax.fori_loop(0, groups, one, 0)

    def directions(c):
        def one(s, carry):
            gradient = grads[s]
            wide = gradient.astype(jnp.float32)
            square = jnp.sum(wide * wide, axis=(0, 1), keepdims=True)
            left_part = jnp.dot(
                root_use[0], gradient, preferred_element_type=jnp.float32
            ).astype(jnp.bfloat16)
            direction = jnp.dot(left_part, root_use[1], preferred_element_type=jnp.float32)
            direction_square = jnp.sum(direction * direction, axis=(0, 1), keepdims=True)
            area = float(width * width)
            ratio = (
                clip_of(s)
                * jnp.sqrt(square / area)
                / jnp.sqrt(direction_square / area + GRAFT_EPSILON)
            )
            outs[s] = (ratio * direction).astype(jnp.bfloat16)
            return carry

        lax.fori_loop(c * chunk_steps, (c + 1) * chunk_steps, one, 0)

        def sort(g, carry):
            split_by_device(c, g, outs, back_stage)
            return carry

        lax.fori_loop(0, groups, sort, 0)

        def send(k, carry):
            d = peer(k)
            copy(
                back_stage.at[c, d], back[c].at[me], send_back.at[c], recv_back.at[c], d
            ).start()
            return carry

        lax.fori_loop(1, holders, send, 0)
        back[c][me] = back_stage[c, me]

    gather_steps(0)
    wait_bytes(roots_d, holders - 1, recv_tile.at[1])
    root_use[0] = jnp.where(has_first > 0, left_roots[0], matrix_of(roots_d, 0))
    root_use[1] = jnp.where(has_first > 0, right_roots[0], matrix_of(roots_d, half))
    for c in range(CHUNKS - 1):
        directions(c)
        gather_steps(c + 1)

    gram_sum[...] = jnp.zeros_like(gram_sum)

    def add_gram(s, carry):
        gradient = grads[s]
        clip = clip_of(s)
        weight = (1.0 - SECOND_MOMENT) * clip * clip / width
        left = lax.dot_general(
            gradient, gradient, (((1,), (1,)), ((), ())), preferred_element_type=jnp.float32
        )
        right = lax.dot_general(
            gradient, gradient, (((0,), (0,)), ((), ())), preferred_element_type=jnp.float32
        )
        gram_sum[0] = SECOND_MOMENT * gram_sum[0] + weight * left
        gram_sum[1] = SECOND_MOMENT * gram_sum[1] + weight * right
        return carry

    lax.fori_loop(0, steps, add_gram, 0)
    tiles_of(gram_sum[0].astype(jnp.bfloat16), grams_a, 0)
    tiles_of(gram_sum[1].astype(jnp.bfloat16), grams_a, half)
    send_tiles(grams_a, grams_b, 2)
    directions(CHUNKS - 1)

    kept = SECOND_MOMENT**steps
    left_out[0] = jnp.where(has_first > 0, kept * left_stats[0] + gram_sum[0], left_stats[0])
    right_out[0] = jnp.where(has_first > 0, kept * right_stats[0] + gram_sum[1], right_stats[0])

    wait_bytes(grams_b, holders - 1, recv_tile.at[2])
    pass_tiles(grams_b, grams_c, grams_d, 3, 3)

    def finish(c):
        wait_bytes(back[c], holders - 1, recv_back.at[c])

        def one(g, carry):
            values = jnp.concatenate(
                [back[c][table[1, g * group + i]] for i in range(group)], axis=0
            )
            done = permute(together, values).reshape(chunk_steps, span, width)
            y_ref[pl.ds(c * chunk_steps, chunk_steps), pl.ds(g * span, span), :] = done
            return carry

        lax.fori_loop(0, groups, one, 0)

    for c in range(CHUNKS):
        finish(c)

    wait_bytes(grams_d, holders - 1, recv_tile.at[3])
    left_new = kept * left_stats[1] + matrix_of(grams_d, 0).astype(jnp.float32)
    right_new = kept * right_stats[1] + matrix_of(grams_d, half).astype(jnp.float32)
    left_out[1] = jnp.where(has_second > 0, left_new, left_stats[1])
    right_out[1] = jnp.where(has_second > 0, right_new, right_stats[1])

    wait_bytes(sums_y, shards - 1, send_y)
    wait_bytes(sums_dp, holders - 1, send_dp)
    for which in range(4):
        wait_bytes(roots_a, holders - 1, send_tile.at[which])
    for c in range(CHUNKS):
        wait_bytes(stage.at[c], holders - 1, send_go.at[c])
        wait_bytes(back_stage.at[c], holders - 1, send_back.at[c])


def shards_step(gradients, owners, left_stats, right_stats, left_roots, right_roots):
    steps, blocks, piece, width = gradients.shape
    holders = lax.axis_size("dp")
    shards = lax.axis_size("tensor")
    rows = piece * (steps // CHUNKS)
    total_count = float(holders * shards * blocks * piece * width)
    table = routes(owners)
    bf16, f32 = jnp.bfloat16, jnp.float32
    message = pltpu.VMEM((CHUNKS, blocks, rows, width), bf16)
    arrivals = pltpu.VMEM((blocks, rows, width), bf16)
    by_step = pltpu.VMEM((steps, width, width), bf16)
    tiles = pltpu.VMEM((holders, TILE_ROWS, TILE_COLS), bf16)
    dma = pltpu.SemaphoreType.DMA
    vmem = pl.BlockSpec(memory_space=pltpu.VMEM)
    sizes = (steps, holders, shards, piece, width, total_count)
    y, left, right = pl.pallas_call(
        functools.partial(kernel, sizes),
        name="shampoo",
        out_shape=(
            jax.ShapeDtypeStruct((steps, blocks * piece, width), bf16),
            jax.ShapeDtypeStruct(left_stats.shape, f32),
            jax.ShapeDtypeStruct(right_stats.shape, f32),
        ),
        in_specs=[pl.BlockSpec(memory_space=pltpu.SMEM)] + [vmem] * 5,
        out_specs=(vmem,) * 3,
        scratch_shapes=[
            message,
            message,
            message,
            by_step,
            by_step,
            message,
            arrivals,
            arrivals,
            tiles,
            tiles,
            tiles,
            tiles,
            tiles,
            tiles,
            tiles,
            tiles,
            pltpu.VMEM((2, width, width), bf16),
            pltpu.VMEM((2, width, width), f32),
            pltpu.VMEM((shards, 1, TILE_COLS), f32),
            pltpu.VMEM((holders, 1, TILE_COLS), f32),
            dma,
            dma,
            dma,
            dma,
            dma((4,)),
            dma((4,)),
            dma((CHUNKS,)),
            dma((CHUNKS,)),
            dma((CHUNKS,)),
            dma((CHUNKS,)),
        ],
        compiler_params=pltpu.CompilerParams(
            collective_id=0, has_side_effects=True, vmem_limit_bytes=40 << 20
        ),
    )(
        table,
        gradients.reshape(steps, blocks * piece, width),
        left_stats,
        right_stats,
        left_roots,
        right_roots,
    )
    return y.reshape(gradients.shape), left, right


def solution(mesh):
    in_specs = (
        P(None, "tensor", "dp", None),
        P("tensor"),
        P(("dp", "tensor"), None, None),
        P(("dp", "tensor"), None, None),
        P(("dp", "tensor"), None, None),
        P(("dp", "tensor"), None, None),
    )
    out_specs = (
        P(None, "tensor", "dp", None),
        P(("dp", "tensor"), None, None),
        P(("dp", "tensor"), None, None),
    )
    return jax.shard_map(
        shards_step, mesh=mesh, in_specs=in_specs, out_specs=out_specs, check_vma=False
    )
```

```python
import functools

import jax
import jax.numpy as jnp
from jax import lax
from jax.experimental import pallas as pl
from jax.experimental.pallas import tpu as pltpu
from jax.sharding import PartitionSpec as P

SECOND_MOMENT = 0.95
CLIP_EPSILON = 1e-06
GRAFT_EPSILON = 1e-06
MESH = pl.DeviceIdType.MESH

CHUNKS = 2
TILE_ROWS, TILE_COLS = 16, 128


def routes(owners):
    count = owners.shape[0]
    position = jnp.arange(count, dtype=jnp.int32)
    same_owner = owners[:, None] == owners[None, :]
    earlier = position[None, :] < position[:, None]
    slot = jnp.sum((same_owner & earlier).astype(jnp.int32), axis=1)
    owned = owners[None, :] == position[:, None]
    first = owned & (slot == 0)[None, :]
    second = owned & (slot == 1)[None, :]
    has_first = jnp.any(first, axis=1)
    has_second = jnp.any(second, axis=1)
    first_block = jnp.sum(jnp.where(first, position[None, :], 0), axis=1)
    second_block = jnp.sum(jnp.where(second, position[None, :], 0), axis=1)
    before = position[None, :] < position[:, None]
    empty_rank = jnp.sum((before & ~has_first[None, :]).astype(jnp.int32), axis=1)
    second_rank = jnp.sum((before & has_second[None, :]).astype(jnp.int32), axis=1)
    match = (
        (empty_rank[:, None] == second_rank[None, :])
        & ~has_first[:, None]
        & has_second[None, :]
    )
    helped = jnp.sum(jnp.where(match, position[None, :], 0), axis=1)
    helper = jnp.sum(jnp.where(match, position[:, None], 0), axis=0)
    helped_block = jnp.sum(jnp.where(match, second_block[None, :], 0), axis=1)
    block_of = jnp.where(has_first, first_block, helped_block)
    device_of = jnp.sum(
        jnp.where(block_of[:, None] == position[None, :], position[:, None], 0), axis=0
    )
    return jnp.stack(
        [
            block_of,
            device_of,
            helped,
            helper,
            has_first.astype(jnp.int32),
            has_second.astype(jnp.int32),
        ]
    )


def kernel(
    sizes,
    table,
    x_ref,
    left_hbm,
    right_hbm,
    y_ref,
    left_delta,
    right_delta,
    left_roots,
    right_roots,
    byblock,
    stage,
    land,
    grads,
    outs,
    back_stage,
    back_first,
    back_second,
    roots_a,
    roots_b,
    roots_c,
    roots_d,
    grams_a,
    grams_b,
    grams_c,
    grams_d,
    root_use,
    sums_y,
    sums_dp,
    send_y,
    recv_y,
    send_dp,
    recv_dp,
    send_tile,
    recv_tile,
    send_go,
    recv_go,
    send_back,
    recv_back,
    load_sem,
):
    steps, holders, shards, piece, width, total_count = sizes
    back = (back_first, back_second)
    chunk_steps = steps // CHUNKS
    rows = piece * chunk_steps
    group = width // rows
    groups = holders // group
    span = group * piece
    me = lax.axis_index("dp")
    shard = lax.axis_index("tensor")

    def peer(k):
        return lax.rem(me + k, holders)

    barrier = pltpu.get_barrier_semaphore()

    def greet(k, carry):
        pl.semaphore_signal(barrier, inc=1, device_id=(peer(k), shard), device_id_type=MESH)
        return carry

    def greet_shard(k, carry):
        pl.semaphore_signal(
            barrier, inc=1, device_id=(me, lax.rem(shard + k, shards)), device_id_type=MESH
        )
        return carry

    lax.fori_loop(1, shards, greet_shard, 0)
    lax.fori_loop(1, holders, greet, 0)

    loads = (
        pltpu.make_async_copy(left_hbm, left_roots, load_sem.at[0]),
        pltpu.make_async_copy(right_hbm, right_roots, load_sem.at[1]),
    )
    for load in loads:
        load.start()

    lane = lax.broadcasted_iota(jnp.int32, (1, TILE_COLS), 1)

    def add_square(s, row):
        values = x_ref[s].astype(jnp.float32)
        square = jnp.sum(values * values, axis=(0, 1), keepdims=True)
        return row + jnp.where(lane == s, square, 0.0)

    local_row = lax.fori_loop(0, steps, add_square, jnp.zeros((1, TILE_COLS), jnp.float32))
    sums_y[pl.ds(shard, 1)] = local_row[None]

    out_index = lax.broadcasted_iota(jnp.int32, (width, width), 0)
    in_index = lax.broadcasted_iota(jnp.int32, (width, width), 1)

    def by_device(index):
        step, rest = index // span, index % span
        return (rest // piece) * rows + step * piece + rest % piece

    apart = (out_index == by_device(in_index)).astype(jnp.bfloat16)
    together = (by_device(out_index) == in_index).astype(jnp.bfloat16)

    def permute(matrix, values):
        return jnp.dot(matrix, values, preferred_element_type=jnp.float32).astype(jnp.bfloat16)

    def split_by_device(c, g, source, target):
        part = source[pl.ds(c * chunk_steps, chunk_steps), pl.ds(g * span, span), :]
        done = permute(apart, part.reshape(width, width))
        target[c, pl.ds(g * group, group)] = done.reshape(group, rows, width)

    def prepare(i, carry):
        split_by_device(i // groups, i % groups, x_ref, byblock)
        return carry

    lax.fori_loop(0, CHUNKS * groups, prepare, 0)

    middle = width // 2
    quarter = middle // TILE_ROWS
    half = 2 * quarter
    last = 2 * half
    down = lax.broadcasted_iota(jnp.int32, (middle, middle), 0)
    across = lax.broadcasted_iota(jnp.int32, (middle, middle), 1)

    def pack(matrix, target, base):
        upper_left = matrix[:middle, :middle].astype(jnp.float32)
        lower_right = matrix[middle:, middle:].astype(jnp.float32)
        mixed = jnp.where(down >= across, upper_left, lower_right).astype(jnp.bfloat16)
        below = matrix[middle:, :middle].astype(jnp.bfloat16)
        target[base : base + quarter] = below.reshape(quarter, TILE_ROWS, middle)
        target[base + quarter : base + half] = mixed.reshape(quarter, TILE_ROWS, middle)
        return jnp.sum(jnp.where(down == across, lower_right, 0.0), axis=0, keepdims=True)

    def pack_pair(left, right, target):
        left_diagonal = pack(left, target, 0)
        right_diagonal = pack(right, target, half)
        row = lax.broadcasted_iota(jnp.int32, (TILE_ROWS, middle), 0)
        target[last] = jnp.where(
            row == 0, left_diagonal, jnp.where(row == 1, right_diagonal, 0.0)
        ).astype(jnp.bfloat16)

    def unpack(source, side):
        base = side * half
        below = source[base : base + quarter].reshape(middle, middle).astype(jnp.float32)
        mixed = source[base + quarter : base + half].reshape(middle, middle).astype(jnp.float32)
        diagonal = source[last].astype(jnp.float32)[side : side + 1, :]
        turned = mixed.T
        upper_left = jnp.where(down >= across, mixed, turned)
        lower_right = jnp.where(
            down < across, mixed, jnp.where(down > across, turned, diagonal)
        )
        return jnp.concatenate(
            [
                jnp.concatenate([upper_left, below.T], axis=1),
                jnp.concatenate([below, lower_right], axis=1),
            ],
            axis=0,
        )

    carries = (lax.rem(me, 2) == 0) | (me == 1)
    mine = jnp.where(me == 1, last, me // 2)

    for load in loads:
        load.wait()
    pack_pair(left_roots[1], right_roots[1], roots_a)

    pl.semaphore_wait(barrier, holders - 1 + shards - 1)

    def copy(source, target, send, recv, device, t=None):
        return pltpu.make_async_remote_copy(
            src_ref=source,
            dst_ref=target,
            send_sem=send,
            recv_sem=recv,
            device_id=(device, shard if t is None else t),
            device_id_type=MESH,
        )

    def wait_bytes(ref, count, semaphore):
        part = ref.at[pl.ds(0, count)]
        pltpu.make_async_copy(part, part, semaphore).wait()

    def send_shard(k, carry):
        t = lax.rem(shard + k, shards)
        copy(sums_y.at[shard], sums_y.at[shard], send_y, recv_y, me, t).start()
        return carry

    lax.fori_loop(1, shards, send_shard, 0)

    def spread_tiles(source, target, which):
        def one(i, carry):
            tile = lax.rem(me // 2 + i, last + 1)
            d = jnp.where(tile == last, 1, 2 * tile)

            @pl.when(d != me)
            def _():
                copy(
                    source.at[tile], target.at[me], send_tile.at[which], recv_tile.at[which], d
                ).start()

            return carry

        lax.fori_loop(0, last + 1, one, 0)

        @pl.when(carries)
        def _():
            target[me] = source[mine]

    def pass_tiles(source, staged, target, which, row):
        @pl.when(carries)
        def _():
            wait_bytes(source, holders - 1, recv_tile.at[which - 1])

            def one(k, carry):
                d = peer(k)
                staged[d] = source[table[row, d]]
                copy(
                    staged.at[d], target.at[mine], send_tile.at[which], recv_tile.at[which], d
                ).start()
                return carry

            lax.fori_loop(1, holders, one, 0)
            target[mine] = source[table[row, me]]

    def wait_tiles(tiles, semaphore):
        @pl.when(carries)
        def _():
            wait_bytes(tiles, last, semaphore)

        @pl.when(jnp.logical_not(carries))
        def _():
            wait_bytes(tiles, last + 1, semaphore)

    spread_tiles(roots_a, roots_b, 0)

    def send_gradients(c):
        def one(k, carry):
            d = peer(k)
            stage[c, d] = byblock[c, table[0, d]]
            copy(stage.at[c, d], land.at[c, me], send_go.at[c], recv_go.at[c], d).start()
            return carry

        lax.fori_loop(1, holders, one, 0)
        land[c, me] = byblock[c, table[0, me]]

    send_gradients(0)

    wait_bytes(sums_y, shards - 1, recv_y)
    shard_row = sums_y[0]
    for t in range(1, shards):
        shard_row = shard_row + sums_y[t]
    sums_dp[pl.ds(me, 1)] = shard_row[None]

    def send_sums(k, carry):
        d = peer(k)
        copy(sums_dp.at[me], sums_dp.at[me], send_dp, recv_dp, d).start()
        return carry

    lax.fori_loop(1, holders, send_sums, 0)

    pass_tiles(roots_b, roots_c, roots_d, 1, 2)

    for c in range(1, CHUNKS):
        send_gradients(c)

    wait_bytes(sums_dp, holders - 1, recv_dp)
    totals = jnp.sum(sums_dp[...], axis=0)
    clip_row = jnp.minimum(1.0, 1.0 / jnp.sqrt(totals / total_count + CLIP_EPSILON))

    def clip_of(s):
        return jnp.sum(jnp.where(lane == s, clip_row, 0.0), axis=1, keepdims=True)

    has_first = table[4, me]

    def gather_steps(c):
        wait_bytes(land.at[c], holders - 1, recv_go.at[c])

        def one(g, carry):
            values = land[c, pl.ds(g * group, group)].reshape(width, width)
            done = permute(together, values).reshape(chunk_steps, span, width)
            grads[pl.ds(c * chunk_steps, chunk_steps), pl.ds(g * span, span), :] = done
            return carry

        lax.fori_loop(0, groups, one, 0)

    def directions(c):
        def one(s, carry):
            gradient = grads[s]
            wide = gradient.astype(jnp.float32)
            square = jnp.sum(wide * wide, axis=(0, 1), keepdims=True)
            left_part = jnp.dot(
                root_use[0], gradient, preferred_element_type=jnp.float32
            ).astype(jnp.bfloat16)
            direction = jnp.dot(left_part, root_use[1], preferred_element_type=jnp.float32)
            direction_square = jnp.sum(direction * direction, axis=(0, 1), keepdims=True)
            area = float(width * width)
            ratio = (
                clip_of(s)
                * jnp.sqrt(square / area)
                / jnp.sqrt(direction_square / area + GRAFT_EPSILON)
            )
            outs[s] = (ratio * direction).astype(jnp.bfloat16)
            return carry

        lax.fori_loop(c * chunk_steps, (c + 1) * chunk_steps, one, 0)

        def sort(g, carry):
            split_by_device(c, g, outs, back_stage)
            return carry

        lax.fori_loop(0, groups, sort, 0)

        def send(k, carry):
            d = peer(k)
            copy(
                back_stage.at[c, d], back[c].at[me], send_back.at[c], recv_back.at[c], d
            ).start()
            return carry

        lax.fori_loop(1, holders, send, 0)
        back[c][me] = back_stage[c, me]

    gather_steps(0)
    wait_tiles(roots_d, recv_tile.at[1])
    for side, own in enumerate((left_roots, right_roots)):
        sent = unpack(roots_d, side).astype(jnp.bfloat16)
        root_use[side] = jnp.where(has_first > 0, own[0], sent)
    for c in range(CHUNKS - 1):
        directions(c)
        gather_steps(c + 1)

    left_delta[0] = jnp.zeros((width, width), jnp.float32)
    right_delta[0] = jnp.zeros((width, width), jnp.float32)

    def add_gram(s, carry):
        gradient = grads[s]
        clip = clip_of(s)
        weight = (1.0 - SECOND_MOMENT) * clip * clip / width
        left = lax.dot_general(
            gradient, gradient, (((1,), (1,)), ((), ())), preferred_element_type=jnp.float32
        )
        right = lax.dot_general(
            gradient, gradient, (((0,), (0,)), ((), ())), preferred_element_type=jnp.float32
        )
        left_delta[0] = SECOND_MOMENT * left_delta[0] + weight * left
        right_delta[0] = SECOND_MOMENT * right_delta[0] + weight * right
        return carry

    lax.fori_loop(0, steps, add_gram, 0)
    pack_pair(left_delta[0], right_delta[0], grams_a)
    spread_tiles(grams_a, grams_b, 2)
    directions(CHUNKS - 1)
    pass_tiles(grams_b, grams_c, grams_d, 3, 3)

    def finish(c):
        wait_bytes(back[c], holders - 1, recv_back.at[c])

        def one(g, carry):
            values = jnp.concatenate(
                [back[c][table[1, g * group + i]] for i in range(group)], axis=0
            )
            done = permute(together, values).reshape(chunk_steps, span, width)
            y_ref[pl.ds(c * chunk_steps, chunk_steps), pl.ds(g * span, span), :] = done
            return carry

        lax.fori_loop(0, groups, one, 0)

    for c in range(CHUNKS):
        finish(c)

    wait_tiles(grams_d, recv_tile.at[3])
    left_delta[1] = unpack(grams_d, 0)
    right_delta[1] = unpack(grams_d, 1)

    wait_bytes(sums_y, shards - 1, send_y)
    wait_bytes(sums_dp, holders - 1, send_dp)
    for which in (0, 2):
        wait_tiles(roots_a, send_tile.at[which])

        @pl.when(carries)
        def _():
            wait_bytes(roots_b, holders - 1, send_tile.at[which + 1])

    for c in range(CHUNKS):
        wait_bytes(stage.at[c], holders - 1, send_go.at[c])
        wait_bytes(back_stage.at[c], holders - 1, send_back.at[c])


def shards_step(gradients, owners, left_stats, right_stats, left_roots, right_roots):
    steps, blocks, piece, width = gradients.shape
    holders = lax.axis_size("dp")
    shards = lax.axis_size("tensor")
    rows = piece * (steps // CHUNKS)
    total_count = float(holders * shards * blocks * piece * width)
    table = routes(owners)
    bf16, f32 = jnp.bfloat16, jnp.float32
    message = pltpu.VMEM((CHUNKS, blocks, rows, width), bf16)
    arrivals = pltpu.VMEM((blocks, rows, width), bf16)
    by_step = pltpu.VMEM((steps, width, width), bf16)
    pieces = 2 * width // TILE_ROWS + 1
    tiles = pltpu.VMEM((pieces, TILE_ROWS, TILE_COLS), bf16)
    gathered = pltpu.VMEM((holders, TILE_ROWS, TILE_COLS), bf16)
    roots = pltpu.VMEM(left_roots.shape, bf16)
    dma = pltpu.SemaphoreType.DMA
    vmem = pl.BlockSpec(memory_space=pltpu.VMEM)
    sizes = (steps, holders, shards, piece, width, total_count)
    y, left_delta, right_delta = pl.pallas_call(
        functools.partial(kernel, sizes),
        name="shampoo",
        out_shape=(
            jax.ShapeDtypeStruct((steps, blocks * piece, width), bf16),
            jax.ShapeDtypeStruct(left_stats.shape, f32),
            jax.ShapeDtypeStruct(right_stats.shape, f32),
        ),
        in_specs=[pl.BlockSpec(memory_space=pltpu.SMEM), vmem] + [pl.BlockSpec(memory_space=pl.ANY)] * 2,
        out_specs=(vmem,) * 3,
        scratch_shapes=[
            roots,
            roots,
            message,
            message,
            message,
            by_step,
            by_step,
            message,
            arrivals,
            arrivals,
            tiles,
            gathered,
            gathered,
            tiles,
            tiles,
            gathered,
            gathered,
            tiles,
            pltpu.VMEM((2, width, width), bf16),
            pltpu.VMEM((shards, 1, TILE_COLS), f32),
            pltpu.VMEM((holders, 1, TILE_COLS), f32),
            dma,
            dma,
            dma,
            dma,
            dma((4,)),
            dma((4,)),
            dma((CHUNKS,)),
            dma((CHUNKS,)),
            dma((CHUNKS,)),
            dma((CHUNKS,)),
            dma((2,)),
        ],
        compiler_params=pltpu.CompilerParams(
            collective_id=0, has_side_effects=True, vmem_limit_bytes=40 << 20
        ),
    )(
        table,
        gradients.reshape(steps, blocks * piece, width),
        left_roots,
        right_roots,
    )
    live = table[4:6, lax.axis_index("dp")][:, None, None] > 0
    kept = SECOND_MOMENT**steps
    left = jnp.where(live, kept * left_stats + left_delta, left_stats)
    right = jnp.where(live, kept * right_stats + right_delta, right_stats)
    return y.reshape(gradients.shape), left, right


def solution(mesh):
    in_specs = (
        P(None, "tensor", "dp", None),
        P("tensor"),
        P(("dp", "tensor"), None, None),
        P(("dp", "tensor"), None, None),
        P(("dp", "tensor"), None, None),
        P(("dp", "tensor"), None, None),
    )
    out_specs = (
        P(None, "tensor", "dp", None),
        P(("dp", "tensor"), None, None),
        P(("dp", "tensor"), None, None),
    )
    return jax.shard_map(
        shards_step, mesh=mesh, in_specs=in_specs, out_specs=out_specs, check_vma=False
    )
```

```python
import functools

import jax
import jax.numpy as jnp
from jax import lax
from jax.experimental import pallas as pl
from jax.experimental.pallas import tpu as pltpu
from jax.sharding import PartitionSpec as P

SECOND_MOMENT = 0.95
CLIP_EPSILON = 1e-06
GRAFT_EPSILON = 1e-06
MESH = pl.DeviceIdType.MESH

CHUNKS = 2
VMEM_BYTES = 56 << 20
TILE_ROWS, TILE_COLS = 16, 128


def routes(owner_row):
    count = owner_row.shape[1]
    down = lax.broadcasted_iota(jnp.int32, (count, count), 0)
    across = lax.broadcasted_iota(jnp.int32, (count, count), 1)

    def along(mask, value, axis):
        return jnp.sum(jnp.where(mask, value, 0), axis=axis, keepdims=True)

    def column(row):
        return along(down == across, row, 1)

    def row(col):
        return along(down == across, col, 0)

    slot = along((column(owner_row) == owner_row) & (down < across), 1, 0)
    owned = owner_row == down
    load = along(owned, 1, 1)
    load_row = row(load)
    first_block = along(owned & (slot == 0), across, 1)
    second_block = along(owned & (slot == 1), across, 1)
    empty_rank = along((across < down) & (load_row == 0), 1, 1)
    second_rank = along((down < across) & (load > 1), 1, 0)
    match = (empty_rank == second_rank) & (load == 0) & (load_row > 1)
    helped = along(match, across, 1)
    helper = along(match, down, 0)
    helped_block = along(match, row(second_block), 1)
    block_of = jnp.where(load > 0, first_block, helped_block)
    device_of = along(block_of == across, down, 0)
    tables = (row(block_of), device_of, row(helped), helper)
    return tuple(jnp.minimum(table, count - 1) for table in tables) + (load_row,)


def kernel(
    sizes,
    owners_hbm,
    x_hbm,
    left_hbm,
    right_hbm,
    left_old_hbm,
    right_old_hbm,
    y_hbm,
    left_new_hbm,
    right_new_hbm,
    y_ref,
    left_new,
    right_new,
    left_old,
    right_old,
    owners_ref,
    table_ref,
    table,
    x_ref,
    left_roots,
    right_roots,
    byblock,
    stage,
    land,
    grads,
    outs,
    back_stage,
    back_first,
    back_second,
    roots_a,
    roots_b,
    roots_c,
    roots_d,
    grams_a,
    grams_b,
    grams_c,
    grams_d,
    root_use,
    sums_y,
    sums_dp,
    send_y,
    recv_y,
    send_dp,
    recv_dp,
    send_tile,
    recv_tile,
    send_go,
    recv_go,
    send_back,
    recv_back,
    load_sem,
    store_sem,
):
    steps, holders, shards, piece, width, total_count = sizes
    back = (back_first, back_second)
    chunk_steps = steps // CHUNKS
    rows = piece * chunk_steps
    group = width // rows
    groups = holders // group
    span = group * piece
    me = lax.axis_index("dp")
    shard = lax.axis_index("tensor")

    def peer(k):
        return lax.rem(me + k, holders)

    barrier = pltpu.get_barrier_semaphore()

    def greet(k, carry):
        pl.semaphore_signal(barrier, inc=1, device_id=(peer(k), shard), device_id_type=MESH)
        return carry

    def greet_shard(k, carry):
        pl.semaphore_signal(
            barrier, inc=1, device_id=(me, lax.rem(shard + k, shards)), device_id_type=MESH
        )
        return carry

    lax.fori_loop(1, shards, greet_shard, 0)
    lax.fori_loop(1, holders, greet, 0)

    loads = [
        pltpu.make_async_copy(source, target, load_sem.at[i])
        for i, (source, target) in enumerate(
            (
                (left_hbm, left_roots),
                (right_hbm, right_roots),
                (owners_hbm, owners_ref),
                (x_hbm, x_ref),
                (left_old_hbm, left_old),
                (right_old_hbm, right_old),
            )
        )
    ]
    for load in loads:
        load.start()

    out_index = lax.broadcasted_iota(jnp.int32, (width, width), 0)
    in_index = lax.broadcasted_iota(jnp.int32, (width, width), 1)

    def by_device(index):
        step, rest = index // span, index % span
        return (rest // piece) * rows + step * piece + rest % piece

    apart = (out_index == by_device(in_index)).astype(jnp.bfloat16)
    together = (by_device(out_index) == in_index).astype(jnp.bfloat16)

    def permute(matrix, values):
        return jnp.dot(matrix, values, preferred_element_type=jnp.float32).astype(jnp.bfloat16)

    def split_by_device(part):
        return jnp.dot(
            apart, part.reshape(width, width), preferred_element_type=jnp.float32
        ).reshape(group, rows, width)

    middle = width // 2
    quarter = middle // TILE_ROWS
    half = 2 * quarter
    last = 2 * half
    down = lax.broadcasted_iota(jnp.int32, (middle, middle), 0)
    across = lax.broadcasted_iota(jnp.int32, (middle, middle), 1)

    def pack(matrix, target, base):
        upper_left = matrix[:middle, :middle].astype(jnp.float32)
        lower_right = matrix[middle:, middle:].astype(jnp.float32)
        mixed = jnp.where(down >= across, upper_left, lower_right).astype(jnp.bfloat16)
        below = matrix[middle:, :middle].astype(jnp.bfloat16)
        target[base : base + quarter] = below.reshape(quarter, TILE_ROWS, middle)
        target[base + quarter : base + half] = mixed.reshape(quarter, TILE_ROWS, middle)
        return jnp.sum(jnp.where(down == across, lower_right, 0.0), axis=0, keepdims=True)

    def pack_pair(left, right, target):
        left_diagonal = pack(left, target, 0)
        right_diagonal = pack(right, target, half)
        row = lax.broadcasted_iota(jnp.int32, (TILE_ROWS, middle), 0)
        target[last] = jnp.where(
            row == 0, left_diagonal, jnp.where(row == 1, right_diagonal, 0.0)
        ).astype(jnp.bfloat16)

    def unpack(source, side):
        base = side * half
        below = source[base : base + quarter].reshape(middle, middle).astype(jnp.float32)
        mixed = source[base + quarter : base + half].reshape(middle, middle).astype(jnp.float32)
        diagonal = source[last].astype(jnp.float32)[side : side + 1, :]
        turned = mixed.T
        upper_left = jnp.where(down >= across, mixed, turned)
        lower_right = jnp.where(
            down < across, mixed, jnp.where(down > across, turned, diagonal)
        )
        return jnp.concatenate(
            [
                jnp.concatenate([upper_left, below.T], axis=1),
                jnp.concatenate([below, lower_right], axis=1),
            ],
            axis=0,
        )

    carries = (lax.rem(me, 2) == 0) | (me == 1)
    mine = jnp.where(me == 1, last, me // 2)

    loads[0].wait()
    loads[1].wait()
    pack_pair(left_roots[1], right_roots[1], roots_a)
    loads[2].wait()
    table_ref[...] = jnp.zeros_like(table_ref)
    for i, values in enumerate(routes(owners_ref[...])):
        table_ref[i : i + 1, :holders] = values
    table_copy = pltpu.make_async_copy(table_ref, table, load_sem.at[6])
    table_copy.start()
    loads[3].wait()

    lane = lax.broadcasted_iota(jnp.int32, (rows, TILE_COLS), 1)
    step_of = lax.broadcasted_iota(jnp.int32, (rows, TILE_COLS), 0) // piece
    local_row = jnp.zeros((1, TILE_COLS), jnp.float32)
    for c in range(CHUNKS):

        def prepare(g, total, c=c):
            part = x_ref[pl.ds(c * chunk_steps, chunk_steps), pl.ds(g * group, group)]
            done = split_by_device(part)
            byblock[c, pl.ds(g * group, group)] = done.astype(jnp.bfloat16)
            return total + jnp.sum(done * done, axis=0)

        squares = lax.fori_loop(0, groups, prepare, jnp.zeros((rows, width), jnp.float32))
        by_row = jnp.sum(squares, axis=1, keepdims=True)
        spot = lane == step_of + c * chunk_steps
        local_row = local_row + jnp.sum(jnp.where(spot, by_row, 0.0), axis=0, keepdims=True)
    sums_y[pl.ds(shard, 1)] = local_row[None]

    pl.semaphore_wait(barrier, holders - 1 + shards - 1)

    def copy(source, target, send, recv, device, t=None):
        return pltpu.make_async_remote_copy(
            src_ref=source,
            dst_ref=target,
            send_sem=send,
            recv_sem=recv,
            device_id=(device, shard if t is None else t),
            device_id_type=MESH,
        )

    def wait_bytes(ref, count, semaphore):
        part = ref.at[pl.ds(0, count)]
        pltpu.make_async_copy(part, part, semaphore).wait()

    def send_shard(k, carry):
        t = lax.rem(shard + k, shards)
        copy(sums_y.at[shard], sums_y.at[shard], send_y, recv_y, me, t).start()
        return carry

    lax.fori_loop(1, shards, send_shard, 0)

    def spread_tiles(source, target, which):
        def one(i, carry):
            tile = lax.rem(me // 2 + i, last + 1)
            d = jnp.where(tile == last, 1, 2 * tile)

            @pl.when(d != me)
            def _():
                copy(
                    source.at[tile], target.at[me], send_tile.at[which], recv_tile.at[which], d
                ).start()

            return carry

        lax.fori_loop(0, last + 1, one, 0)

        @pl.when(carries)
        def _():
            target[me] = source[mine]

    def pass_tiles(source, staged, target, which, row):
        @pl.when(carries)
        def _():
            wait_bytes(source, holders - 1, recv_tile.at[which - 1])

            def one(k, carry):
                d = peer(k)
                staged[d] = source[table[row, d]]
                copy(
                    staged.at[d], target.at[mine], send_tile.at[which], recv_tile.at[which], d
                ).start()
                return carry

            lax.fori_loop(1, holders, one, 0)
            target[mine] = source[table[row, me]]

    def wait_tiles(tiles, semaphore):
        @pl.when(carries)
        def _():
            wait_bytes(tiles, last, semaphore)

        @pl.when(jnp.logical_not(carries))
        def _():
            wait_bytes(tiles, last + 1, semaphore)

    spread_tiles(roots_a, roots_b, 0)

    table_copy.wait()

    def send_gradients(c):
        def one(k, carry):
            d = peer(k)
            stage[c, d] = byblock[c, table[0, d]]
            copy(stage.at[c, d], land.at[c, me], send_go.at[c], recv_go.at[c], d).start()
            return carry

        lax.fori_loop(1, holders, one, 0)
        land[c, me] = byblock[c, table[0, me]]

    send_gradients(0)

    wait_bytes(sums_y, shards - 1, recv_y)
    shard_row = sums_y[0]
    for t in range(1, shards):
        shard_row = shard_row + sums_y[t]
    sums_dp[pl.ds(me, 1)] = shard_row[None]

    def send_sums(k, carry):
        d = peer(k)
        copy(sums_dp.at[me], sums_dp.at[me], send_dp, recv_dp, d).start()
        return carry

    lax.fori_loop(1, holders, send_sums, 0)

    pass_tiles(roots_b, roots_c, roots_d, 1, 2)

    for c in range(1, CHUNKS):
        send_gradients(c)

    wait_bytes(sums_dp, holders - 1, recv_dp)
    totals = jnp.sum(sums_dp[...], axis=0)
    clip_row = jnp.minimum(1.0, 1.0 / jnp.sqrt(totals / total_count + CLIP_EPSILON))

    def clip_of(s):
        return jnp.sum(jnp.where(lane[:1] == s, clip_row, 0.0), axis=1, keepdims=True)

    load = table[4, me]

    def gather_steps(c):
        wait_bytes(land.at[c], holders - 1, recv_go.at[c])

        def one(g, carry):
            values = land[c, pl.ds(g * group, group)].reshape(width, width)
            done = permute(together, values).reshape(chunk_steps, span, width)
            grads[pl.ds(c * chunk_steps, chunk_steps), pl.ds(g * span, span), :] = done
            return carry

        lax.fori_loop(0, groups, one, 0)

    def directions(c):
        def one(s, carry):
            gradient = grads[s]
            wide = gradient.astype(jnp.float32)
            square = jnp.sum(wide * wide, axis=(0, 1), keepdims=True)
            left_part = jnp.dot(
                root_use[0], gradient, preferred_element_type=jnp.float32
            ).astype(jnp.bfloat16)
            direction = jnp.dot(left_part, root_use[1], preferred_element_type=jnp.float32)
            direction_square = jnp.sum(direction * direction, axis=(0, 1), keepdims=True)
            area = float(width * width)
            ratio = (
                clip_of(s)
                * jnp.sqrt(square / area)
                / jnp.sqrt(direction_square / area + GRAFT_EPSILON)
            )
            outs[s] = (ratio * direction).astype(jnp.bfloat16)
            return carry

        lax.fori_loop(c * chunk_steps, (c + 1) * chunk_steps, one, 0)

        def sort(g, carry):
            part = outs[pl.ds(c * chunk_steps, chunk_steps), pl.ds(g * span, span), :]
            back_stage[c, pl.ds(g * group, group)] = split_by_device(part).astype(jnp.bfloat16)
            return carry

        lax.fori_loop(0, groups, sort, 0)

        def send(k, carry):
            d = peer(k)
            copy(
                back_stage.at[c, d], back[c].at[me], send_back.at[c], recv_back.at[c], d
            ).start()
            return carry

        lax.fori_loop(1, holders, send, 0)
        back[c][me] = back_stage[c, me]

    gather_steps(0)
    wait_tiles(roots_d, recv_tile.at[1])
    for side, own in enumerate((left_roots, right_roots)):
        sent = unpack(roots_d, side).astype(jnp.bfloat16)
        root_use[side] = jnp.where(load > 0, own[0], sent)
    for c in range(CHUNKS - 1):
        directions(c)
        gather_steps(c + 1)

    left_new[0] = jnp.zeros((width, width), jnp.float32)
    right_new[0] = jnp.zeros((width, width), jnp.float32)

    def add_gram(s, carry):
        gradient = grads[s]
        clip = clip_of(s)
        weight = (1.0 - SECOND_MOMENT) * clip * clip / width
        left = lax.dot_general(
            gradient, gradient, (((1,), (1,)), ((), ())), preferred_element_type=jnp.float32
        )
        right = lax.dot_general(
            gradient, gradient, (((0,), (0,)), ((), ())), preferred_element_type=jnp.float32
        )
        left_new[0] = SECOND_MOMENT * left_new[0] + weight * left
        right_new[0] = SECOND_MOMENT * right_new[0] + weight * right
        return carry

    lax.fori_loop(0, steps, add_gram, 0)
    pack_pair(left_new[0], right_new[0], grams_a)
    spread_tiles(grams_a, grams_b, 2)
    directions(CHUNKS - 1)

    kept = SECOND_MOMENT**steps
    stores = []

    def store(source, target):
        done = pltpu.make_async_copy(source, target, store_sem.at[len(stores)])
        done.start()
        stores.append(done)

    sides = ((left_old, left_new, left_new_hbm), (right_old, right_new, right_new_hbm))
    for side, (old, new, target) in enumerate(sides):
        loads[4 + side].wait()
        new[0] = jnp.where(load > 0, kept * old[0] + new[0], old[0])
        store(new.at[0], target.at[0])

    pass_tiles(grams_b, grams_c, grams_d, 3, 3)

    def finish(c):
        wait_bytes(back[c], holders - 1, recv_back.at[c])

        def one(g, carry):
            values = jnp.concatenate(
                [back[c][table[1, g * group + i]] for i in range(group)], axis=0
            )
            done = permute(together, values).reshape(chunk_steps, group, piece, width)
            y_ref[pl.ds(c * chunk_steps, chunk_steps), pl.ds(g * group, group)] = done
            return carry

        lax.fori_loop(0, groups, one, 0)
        part = pl.ds(c * chunk_steps, chunk_steps)
        store(y_ref.at[part], y_hbm.at[part])

    for c in range(CHUNKS):
        finish(c)

    wait_tiles(grams_d, recv_tile.at[3])
    for side, (old, new, target) in enumerate(sides):
        new[1] = jnp.where(load > 1, kept * old[1] + unpack(grams_d, side), old[1])
        store(new.at[1], target.at[1])

    wait_bytes(sums_y, shards - 1, send_y)
    wait_bytes(sums_dp, holders - 1, send_dp)
    for which in (0, 2):
        wait_tiles(roots_a, send_tile.at[which])

        @pl.when(carries)
        def _():
            wait_bytes(roots_b, holders - 1, send_tile.at[which + 1])

    for c in range(CHUNKS):
        wait_bytes(stage.at[c], holders - 1, send_go.at[c])
        wait_bytes(back_stage.at[c], holders - 1, send_back.at[c])
    for done in stores:
        done.wait()


def hand_over(count, *refs):
    inputs, outputs, rooms = refs[:count], refs[count : 2 * count], refs[2 * count : 3 * count]
    load_sem, store_sem = refs[3 * count :]
    parts = [(k, i) for k in range(count) for i in range(inputs[k].shape[0])]
    loads, stores = [], []
    for n, (k, i) in enumerate(parts):
        loads.append(pltpu.make_async_copy(inputs[k].at[i], rooms[k].at[i], load_sem.at[n]))
        stores.append(pltpu.make_async_copy(rooms[k].at[i], outputs[k].at[i], store_sem.at[n]))
    for load in loads:
        load.start()
    for load, store in zip(loads, stores):
        load.wait()
        store.start()
    for store in stores:
        store.wait()


def shards_step(gradients, owners, left_stats, right_stats, left_roots, right_roots):
    steps, blocks, piece, width = gradients.shape
    holders = lax.axis_size("dp")
    shards = lax.axis_size("tensor")
    rows = piece * (steps // CHUNKS)
    total_count = float(holders * shards * blocks * piece * width)
    bf16, f32 = jnp.bfloat16, jnp.float32
    message = pltpu.VMEM((CHUNKS, blocks, rows, width), bf16)
    arrivals = pltpu.VMEM((blocks, rows, width), bf16)
    by_step = pltpu.VMEM((steps, width, width), bf16)
    pieces = 2 * width // TILE_ROWS + 1
    tiles = pltpu.VMEM((pieces, TILE_ROWS, TILE_COLS), bf16)
    gathered = pltpu.VMEM((holders, TILE_ROWS, TILE_COLS), bf16)
    roots = pltpu.VMEM(left_roots.shape, bf16)
    dma = pltpu.SemaphoreType.DMA
    hbm = pl.BlockSpec(memory_space=pl.ANY)
    sizes = (steps, holders, shards, piece, width, total_count)
    outs = (
        jax.ShapeDtypeStruct(gradients.shape, bf16),
        jax.ShapeDtypeStruct(left_stats.shape, f32),
        jax.ShapeDtypeStruct(right_stats.shape, f32),
    )
    stats = pltpu.VMEM(left_stats.shape, f32)
    results = pl.pallas_call(
        functools.partial(kernel, sizes),
        name="shampoo",
        out_shape=outs,
        in_specs=[hbm] * 6,
        out_specs=(hbm,) * 3,
        scratch_shapes=[
            pltpu.VMEM(gradients.shape, bf16),
            stats,
            stats,
            stats,
            stats,
            pltpu.VMEM((1, blocks), jnp.int32),
            pltpu.VMEM((8, TILE_COLS), jnp.int32),
            pltpu.SMEM((8, TILE_COLS), jnp.int32),
            pltpu.VMEM(gradients.shape, bf16),
            roots,
            roots,
            message,
            message,
            message,
            by_step,
            by_step,
            message,
            arrivals,
            arrivals,
            tiles,
            gathered,
            gathered,
            tiles,
            tiles,
            gathered,
            gathered,
            tiles,
            pltpu.VMEM((2, width, width), bf16),
            pltpu.VMEM((shards, 1, TILE_COLS), f32),
            pltpu.VMEM((holders, 1, TILE_COLS), f32),
            dma,
            dma,
            dma,
            dma,
            dma((4,)),
            dma((4,)),
            dma((CHUNKS,)),
            dma((CHUNKS,)),
            dma((CHUNKS,)),
            dma((CHUNKS,)),
            dma((7,)),
            dma((CHUNKS + 4,)),
        ],
        compiler_params=pltpu.CompilerParams(
            collective_id=0, has_side_effects=True, vmem_limit_bytes=VMEM_BYTES
        ),
    )(owners.reshape(1, blocks), gradients, left_roots, right_roots, left_stats, right_stats)
    parts = sum(out.shape[0] for out in outs)
    return pl.pallas_call(
        functools.partial(hand_over, len(outs)),
        name="hand_over",
        out_shape=outs,
        in_specs=[hbm] * 3,
        out_specs=(hbm,) * 3,
        scratch_shapes=[pltpu.VMEM(out.shape, out.dtype) for out in outs]
        + [dma((parts,)), dma((parts,))],
        compiler_params=pltpu.CompilerParams(vmem_limit_bytes=VMEM_BYTES),
    )(*results)


def solution(mesh):
    in_specs = (
        P(None, "tensor", "dp", None),
        P("tensor"),
        P(("dp", "tensor"), None, None),
        P(("dp", "tensor"), None, None),
        P(("dp", "tensor"), None, None),
        P(("dp", "tensor"), None, None),
    )
    out_specs = (
        P(None, "tensor", "dp", None),
        P(("dp", "tensor"), None, None),
        P(("dp", "tensor"), None, None),
    )
    return jax.shard_map(
        shards_step, mesh=mesh, in_specs=in_specs, out_specs=out_specs, check_vma=False
    )
```

```python
import functools

import jax
import jax.numpy as jnp
from jax import lax
from jax.experimental import pallas as pl
from jax.experimental.pallas import tpu as pltpu
from jax.sharding import PartitionSpec as P

SECOND_MOMENT = 0.95
CLIP_EPSILON = 1e-06
GRAFT_EPSILON = 1e-06
MESH = pl.DeviceIdType.MESH

CHUNKS = 2
VMEM_BYTES = 56 << 20
TILE_ROWS, TILE_COLS = 16, 128


def routes(owner_row):
    count = owner_row.shape[1]
    down = lax.broadcasted_iota(jnp.int32, (count, count), 0)
    across = lax.broadcasted_iota(jnp.int32, (count, count), 1)

    def along(mask, value, axis):
        return jnp.sum(jnp.where(mask, value, 0), axis=axis, keepdims=True)

    def column(row):
        return along(down == across, row, 1)

    def row(col):
        return along(down == across, col, 0)

    slot = along((column(owner_row) == owner_row) & (down < across), 1, 0)
    owned = owner_row == down
    load = along(owned, 1, 1)
    load_row = row(load)
    first_block = along(owned & (slot == 0), across, 1)
    second_block = along(owned & (slot == 1), across, 1)
    empty_rank = along((across < down) & (load_row == 0), 1, 1)
    second_rank = along((down < across) & (load > 1), 1, 0)
    match = (empty_rank == second_rank) & (load == 0) & (load_row > 1)
    helped = along(match, across, 1)
    helper = along(match, down, 0)
    helped_block = along(match, row(second_block), 1)
    block_of = jnp.where(load > 0, first_block, helped_block)
    device_of = along(block_of == across, down, 0)
    tables = (row(block_of), device_of, row(helped), helper)
    return tuple(jnp.minimum(table, count - 1) for table in tables) + (load_row,)


def kernel(
    sizes,
    owners_hbm,
    x_hbm,
    left_hbm,
    right_hbm,
    left_old_hbm,
    right_old_hbm,
    y_hbm,
    left_new_hbm,
    right_new_hbm,
    y_ref,
    left_new,
    right_new,
    left_old,
    right_old,
    owners_ref,
    table_ref,
    table,
    x_ref,
    left_roots,
    right_roots,
    byblock,
    stage,
    land,
    grads,
    outs,
    back_stage,
    back_first,
    back_second,
    roots_a,
    roots_b,
    roots_c,
    roots_d,
    grams_a,
    grams_b,
    grams_c,
    grams_d,
    diag_a,
    diag_b_roots,
    diag_b_grams,
    diag_c,
    diag_d,
    root_use,
    sums_y,
    sums_dp,
    send_y,
    recv_y,
    send_dp,
    recv_dp,
    send_tile,
    recv_tile,
    send_diag,
    recv_diag,
    send_go,
    recv_go,
    send_back,
    recv_back,
    load_sem,
    store_sem,
):
    steps, holders, shards, piece, width, total_count = sizes
    back = (back_first, back_second)
    chunk_steps = steps // CHUNKS
    rows = piece * chunk_steps
    group = width // rows
    groups = holders // group
    span = group * piece
    me = lax.axis_index("dp")
    shard = lax.axis_index("tensor")

    plane = holders // 8

    def peer(k):
        i = k - 1
        far = i < 7 * plane
        up = jnp.where(far, i % 7 + 1, 0)
        along = jnp.where(far, i // 7, i - 7 * plane + 1)
        return (me // plane + up) % 8 * plane + (me + along) % plane

    barrier = pltpu.get_barrier_semaphore()

    def greet(k, carry):
        pl.semaphore_signal(barrier, inc=1, device_id=(peer(k), shard), device_id_type=MESH)
        return carry

    def greet_shard(k, carry):
        pl.semaphore_signal(
            barrier, inc=1, device_id=(me, lax.rem(shard + k, shards)), device_id_type=MESH
        )
        return carry

    lax.fori_loop(1, shards, greet_shard, 0)
    lax.fori_loop(1, holders, greet, 0)

    loads = [
        pltpu.make_async_copy(source, target, load_sem.at[i])
        for i, (source, target) in enumerate(
            (
                (left_hbm, left_roots),
                (right_hbm, right_roots),
                (owners_hbm, owners_ref),
                (x_hbm, x_ref),
                (left_old_hbm, left_old),
                (right_old_hbm, right_old),
            )
        )
    ]
    for load in loads:
        load.start()

    out_index = lax.broadcasted_iota(jnp.int32, (width, width), 0)
    in_index = lax.broadcasted_iota(jnp.int32, (width, width), 1)

    def by_device(index):
        step, rest = index // span, index % span
        return (rest // piece) * rows + step * piece + rest % piece

    apart = (out_index == by_device(in_index)).astype(jnp.bfloat16)
    together = (by_device(out_index) == in_index).astype(jnp.bfloat16)

    def permute(matrix, values):
        return jnp.dot(matrix, values, preferred_element_type=jnp.float32).astype(jnp.bfloat16)

    def split_by_device(part):
        return jnp.dot(
            apart, part.reshape(width, width), preferred_element_type=jnp.float32
        ).reshape(group, rows, width)

    middle = width // 2
    quarter = middle // TILE_ROWS
    half = 2 * quarter
    count = 2 * half
    diag_b = (diag_b_roots, diag_b_grams)
    down = lax.broadcasted_iota(jnp.int32, (middle, middle), 0)
    across = lax.broadcasted_iota(jnp.int32, (middle, middle), 1)

    def pack(matrix, target, base):
        upper_left = matrix[:middle, :middle].astype(jnp.float32)
        lower_right = matrix[middle:, middle:].astype(jnp.float32)
        mixed = jnp.where(down >= across, upper_left, lower_right).astype(jnp.bfloat16)
        below = matrix[middle:, :middle].astype(jnp.bfloat16)
        target[base : base + quarter] = below.reshape(quarter, TILE_ROWS, middle)
        target[base + quarter : base + half] = mixed.reshape(quarter, TILE_ROWS, middle)
        return jnp.sum(jnp.where(down == across, lower_right, 0.0), axis=0, keepdims=True)

    def pack_pair(left, right, target, kind):
        diag_a[kind, 0] = pack(left, target, 0)
        diag_a[kind, 1] = pack(right, target, half)

    def unpack(source, side, kind):
        base = side * half
        below = source[base : base + quarter].reshape(middle, middle).astype(jnp.float32)
        mixed = source[base + quarter : base + half].reshape(middle, middle).astype(jnp.float32)
        diagonal = diag_d[kind, side]
        turned = mixed.T
        upper_left = jnp.where(down >= across, mixed, turned)
        lower_right = jnp.where(
            down < across, mixed, jnp.where(down > across, turned, diagonal)
        )
        return jnp.concatenate(
            [
                jnp.concatenate([upper_left, below.T], axis=1),
                jnp.concatenate([below, lower_right], axis=1),
            ],
            axis=0,
        )

    carries = lax.rem(me, 2) == 0
    mine = me // 2
    homes = (1, holders // 2 + 1)
    holds = (me == homes[0]) | (me == homes[1])
    my_side = jnp.where(me == homes[1], 1, 0)

    loads[0].wait()
    loads[1].wait()
    pack_pair(left_roots[1], right_roots[1], roots_a, 0)
    loads[2].wait()
    table_ref[...] = jnp.zeros_like(table_ref)
    for i, values in enumerate(routes(owners_ref[...])):
        table_ref[i : i + 1, :holders] = values
    table_copy = pltpu.make_async_copy(table_ref, table, load_sem.at[6])
    table_copy.start()
    loads[3].wait()

    lane = lax.broadcasted_iota(jnp.int32, (rows, TILE_COLS), 1)
    step_of = lax.broadcasted_iota(jnp.int32, (rows, TILE_COLS), 0) // piece
    local_row = jnp.zeros((1, TILE_COLS), jnp.float32)
    for c in range(CHUNKS):

        def prepare(g, total, c=c):
            part = x_ref[pl.ds(c * chunk_steps, chunk_steps), pl.ds(g * group, group)]
            done = split_by_device(part)
            byblock[c, pl.ds(g * group, group)] = done.astype(jnp.bfloat16)
            return total + jnp.sum(done * done, axis=0)

        squares = lax.fori_loop(0, groups, prepare, jnp.zeros((rows, width), jnp.float32))
        by_row = jnp.sum(squares, axis=1, keepdims=True)
        spot = lane == step_of + c * chunk_steps
        local_row = local_row + jnp.sum(jnp.where(spot, by_row, 0.0), axis=0, keepdims=True)
    sums_y[pl.ds(shard, 1)] = local_row[None]

    pl.semaphore_wait(barrier, holders - 1 + shards - 1)

    def copy(source, target, send, recv, device, t=None):
        return pltpu.make_async_remote_copy(
            src_ref=source,
            dst_ref=target,
            send_sem=send,
            recv_sem=recv,
            device_id=(device, shard if t is None else t),
            device_id_type=MESH,
        )

    def wait_bytes(ref, count, semaphore):
        part = ref.at[pl.ds(0, count)]
        pltpu.make_async_copy(part, part, semaphore).wait()

    def send_shard(k, carry):
        t = lax.rem(shard + k, shards)
        copy(sums_y.at[shard], sums_y.at[shard], send_y, recv_y, me, t).start()
        return carry

    lax.fori_loop(1, shards, send_shard, 0)

    def spread_tiles(source, target, which):
        def one(i, carry):
            chips = plane // 2
            far = i < 7 * chips
            up = jnp.where(far, i % 7 + 1, 0)
            along = jnp.where(far, i // 7, i - 7 * chips)
            chip = (me // plane + up) % 8 * chips + (me // 2 + along) % chips
            tile, d = chip, 2 * chip

            @pl.when(d != me)
            def _():
                copy(
                    source.at[tile], target.at[me], send_tile.at[which], recv_tile.at[which], d
                ).start()

            return carry

        lax.fori_loop(0, count, one, 0)

        @pl.when(carries)
        def _():
            target[me] = source[mine]

        kind = which // 2
        for side, d in enumerate(homes):

            @pl.when(me != d)
            def _(side=side, d=d):
                copy(
                    diag_a.at[kind, side],
                    diag_b[kind].at[me],
                    send_diag.at[which],
                    recv_diag.at[which],
                    d,
                ).start()

            @pl.when(me == d)
            def _(side=side):
                diag_b[kind][me] = diag_a[kind, side]

    def pass_tiles(source, staged, target, which, row):
        @pl.when(carries)
        def _():
            wait_bytes(source, holders - 1, recv_tile.at[which - 1])

            def one(k, carry):
                d = peer(k)
                staged[d] = source[table[row, d]]
                copy(
                    staged.at[d], target.at[mine], send_tile.at[which], recv_tile.at[which], d
                ).start()
                return carry

            lax.fori_loop(1, holders, one, 0)
            target[mine] = source[table[row, me]]

        @pl.when(holds)
        def _():
            kind = which // 2
            rows_in = diag_b[kind]
            wait_bytes(rows_in, holders - 1, recv_diag.at[which - 1])

            def one(k, carry):
                d = peer(k)
                diag_c[kind, d] = rows_in[table[row, d]]
                copy(
                    diag_c.at[kind, d],
                    diag_d.at[kind, my_side],
                    send_diag.at[which],
                    recv_diag.at[which],
                    d,
                ).start()
                return carry

            lax.fori_loop(1, holders, one, 0)
            diag_d[kind, my_side] = rows_in[table[row, me]]

    def wait_tiles(tiles, semaphore, diagonal_semaphore):
        @pl.when(carries)
        def _():
            wait_bytes(tiles, count - 1, semaphore)

        @pl.when(jnp.logical_not(carries))
        def _():
            wait_bytes(tiles, count, semaphore)

        @pl.when(holds)
        def _():
            wait_bytes(diag_d.at[0], 1, diagonal_semaphore)

        @pl.when(jnp.logical_not(holds))
        def _():
            wait_bytes(diag_d.at[0], 2, diagonal_semaphore)

    spread_tiles(roots_a, roots_b, 0)

    table_copy.wait()

    def send_gradients(c):
        def one(k, carry):
            d = peer(k)
            stage[c, d] = byblock[c, table[0, d]]
            copy(stage.at[c, d], land.at[c, me], send_go.at[c], recv_go.at[c], d).start()
            return carry

        lax.fori_loop(1, holders, one, 0)
        land[c, me] = byblock[c, table[0, me]]

    send_gradients(0)

    wait_bytes(sums_y, shards - 1, recv_y)
    shard_row = sums_y[0]
    for t in range(1, shards):
        shard_row = shard_row + sums_y[t]
    sums_dp[pl.ds(me, 1)] = shard_row[None]

    def send_sums(k, carry):
        d = peer(k)
        copy(sums_dp.at[me], sums_dp.at[me], send_dp, recv_dp, d).start()
        return carry

    lax.fori_loop(1, holders, send_sums, 0)

    pass_tiles(roots_b, roots_c, roots_d, 1, 2)

    for c in range(1, CHUNKS):
        send_gradients(c)

    wait_bytes(sums_dp, holders - 1, recv_dp)
    totals = jnp.sum(sums_dp[...], axis=0)
    clip_row = jnp.minimum(1.0, 1.0 / jnp.sqrt(totals / total_count + CLIP_EPSILON))

    def clip_of(s):
        return jnp.sum(jnp.where(lane[:1] == s, clip_row, 0.0), axis=1, keepdims=True)

    load = table[4, me]

    def gather_steps(c):
        wait_bytes(land.at[c], holders - 1, recv_go.at[c])

        def one(g, carry):
            values = land[c, pl.ds(g * group, group)].reshape(width, width)
            done = permute(together, values).reshape(chunk_steps, span, width)
            grads[pl.ds(c * chunk_steps, chunk_steps), pl.ds(g * span, span), :] = done
            return carry

        lax.fori_loop(0, groups, one, 0)

    def directions(c):
        def one(s, carry):
            gradient = grads[s]
            wide = gradient.astype(jnp.float32)
            square = jnp.sum(wide * wide, axis=(0, 1), keepdims=True)
            left_part = jnp.dot(
                root_use[0], gradient, preferred_element_type=jnp.float32
            ).astype(jnp.bfloat16)
            direction = jnp.dot(left_part, root_use[1], preferred_element_type=jnp.float32)
            direction_square = jnp.sum(direction * direction, axis=(0, 1), keepdims=True)
            area = float(width * width)
            ratio = (
                clip_of(s)
                * jnp.sqrt(square / area)
                / jnp.sqrt(direction_square / area + GRAFT_EPSILON)
            )
            outs[s] = (ratio * direction).astype(jnp.bfloat16)
            return carry

        lax.fori_loop(c * chunk_steps, (c + 1) * chunk_steps, one, 0)

        def sort(g, carry):
            part = outs[pl.ds(c * chunk_steps, chunk_steps), pl.ds(g * span, span), :]
            back_stage[c, pl.ds(g * group, group)] = split_by_device(part).astype(jnp.bfloat16)
            return carry

        lax.fori_loop(0, groups, sort, 0)

        def send(k, carry):
            d = peer(k)
            copy(
                back_stage.at[c, d], back[c].at[me], send_back.at[c], recv_back.at[c], d
            ).start()
            return carry

        lax.fori_loop(1, holders, send, 0)
        back[c][me] = back_stage[c, me]

    left_new[0] = jnp.zeros((width, width), jnp.float32)
    right_new[0] = jnp.zeros((width, width), jnp.float32)

    def add_gram(s, carry):
        gradient = grads[s]
        clip = clip_of(s)
        weight = (1.0 - SECOND_MOMENT) * clip * clip / width
        left = lax.dot_general(
            gradient, gradient, (((1,), (1,)), ((), ())), preferred_element_type=jnp.float32
        )
        right = lax.dot_general(
            gradient, gradient, (((0,), (0,)), ((), ())), preferred_element_type=jnp.float32
        )
        left_new[0] = SECOND_MOMENT * left_new[0] + weight * left
        right_new[0] = SECOND_MOMENT * right_new[0] + weight * right
        return carry

    def add_grams(c):
        lax.fori_loop(c * chunk_steps, (c + 1) * chunk_steps, add_gram, 0)

    gather_steps(0)
    wait_tiles(roots_d, recv_tile.at[1], recv_diag.at[1])
    for side, own in enumerate((left_roots, right_roots)):
        sent = unpack(roots_d, side, 0).astype(jnp.bfloat16)
        root_use[side] = jnp.where(load > 0, own[0], sent)
    for c in range(CHUNKS - 1):
        directions(c)
        add_grams(c)
        gather_steps(c + 1)
    add_grams(CHUNKS - 1)

    pack_pair(left_new[0], right_new[0], grams_a, 1)
    spread_tiles(grams_a, grams_b, 2)
    directions(CHUNKS - 1)

    kept = SECOND_MOMENT**steps
    stores = []

    def store(source, target):
        done = pltpu.make_async_copy(source, target, store_sem.at[len(stores)])
        done.start()
        stores.append(done)

    sides = ((left_old, left_new, left_new_hbm), (right_old, right_new, right_new_hbm))
    for side, (old, new, target) in enumerate(sides):
        loads[4 + side].wait()
        new[0] = jnp.where(load > 0, kept * old[0] + new[0], old[0])
        store(new.at[0], target.at[0])

    pass_tiles(grams_b, grams_c, grams_d, 3, 3)

    def finish(c):
        wait_bytes(back[c], holders - 1, recv_back.at[c])

        def one(g, carry):
            values = jnp.concatenate(
                [back[c][table[1, g * group + i]] for i in range(group)], axis=0
            )
            done = permute(together, values).reshape(chunk_steps, group, piece, width)
            y_ref[pl.ds(c * chunk_steps, chunk_steps), pl.ds(g * group, group)] = done
            return carry

        lax.fori_loop(0, groups, one, 0)
        part = pl.ds(c * chunk_steps, chunk_steps)
        store(y_ref.at[part], y_hbm.at[part])

    for c in range(CHUNKS):
        finish(c)

    wait_tiles(grams_d, recv_tile.at[3], recv_diag.at[3])
    for side, (old, new, target) in enumerate(sides):
        new[1] = jnp.where(load > 1, kept * old[1] + unpack(grams_d, side, 1), old[1])
        store(new.at[1], target.at[1])

    wait_bytes(sums_y, shards - 1, send_y)
    wait_bytes(sums_dp, holders - 1, send_dp)
    for which in (0, 2):
        wait_tiles(roots_a, send_tile.at[which], send_diag.at[which])

        @pl.when(carries)
        def _():
            wait_bytes(roots_b, holders - 1, send_tile.at[which + 1])

        @pl.when(holds)
        def _():
            wait_bytes(diag_b_roots, holders - 1, send_diag.at[which + 1])

    for c in range(CHUNKS):
        wait_bytes(stage.at[c], holders - 1, send_go.at[c])
        wait_bytes(back_stage.at[c], holders - 1, send_back.at[c])
    for done in stores:
        done.wait()


def hand_over(count, *refs):
    inputs, outputs, rooms = refs[:count], refs[count : 2 * count], refs[2 * count : 3 * count]
    load_sem, store_sem = refs[3 * count :]
    parts = [(k, i) for k in range(count) for i in range(inputs[k].shape[0])]
    loads, stores = [], []
    for n, (k, i) in enumerate(parts):
        loads.append(pltpu.make_async_copy(inputs[k].at[i], rooms[k].at[i], load_sem.at[n]))
        stores.append(pltpu.make_async_copy(rooms[k].at[i], outputs[k].at[i], store_sem.at[n]))
    for load in loads:
        load.start()
    for load, store in zip(loads, stores):
        load.wait()
        store.start()
    for store in stores:
        store.wait()


def shards_step(gradients, owners, left_stats, right_stats, left_roots, right_roots):
    steps, blocks, piece, width = gradients.shape
    holders = lax.axis_size("dp")
    shards = lax.axis_size("tensor")
    rows = piece * (steps // CHUNKS)
    total_count = float(holders * shards * blocks * piece * width)
    bf16, f32 = jnp.bfloat16, jnp.float32
    message = pltpu.VMEM((CHUNKS, blocks, rows, width), bf16)
    arrivals = pltpu.VMEM((blocks, rows, width), bf16)
    by_step = pltpu.VMEM((steps, width, width), bf16)
    pieces = 2 * width // TILE_ROWS
    tiles = pltpu.VMEM((pieces, TILE_ROWS, TILE_COLS), bf16)
    gathered = pltpu.VMEM((holders, TILE_ROWS, TILE_COLS), bf16)
    diagonals = pltpu.VMEM((2, 2, 1, TILE_COLS), f32)
    one_per_device = pltpu.VMEM((holders, 1, TILE_COLS), f32)
    roots = pltpu.VMEM(left_roots.shape, bf16)
    dma = pltpu.SemaphoreType.DMA
    hbm = pl.BlockSpec(memory_space=pl.ANY)
    sizes = (steps, holders, shards, piece, width, total_count)
    outs = (
        jax.ShapeDtypeStruct(gradients.shape, bf16),
        jax.ShapeDtypeStruct(left_stats.shape, f32),
        jax.ShapeDtypeStruct(right_stats.shape, f32),
    )
    stats = pltpu.VMEM(left_stats.shape, f32)
    results = pl.pallas_call(
        functools.partial(kernel, sizes),
        name="shampoo",
        out_shape=outs,
        in_specs=[hbm] * 6,
        out_specs=(hbm,) * 3,
        scratch_shapes=[
            pltpu.VMEM(gradients.shape, bf16),
            stats,
            stats,
            stats,
            stats,
            pltpu.VMEM((1, blocks), jnp.int32),
            pltpu.VMEM((8, TILE_COLS), jnp.int32),
            pltpu.SMEM((8, TILE_COLS), jnp.int32),
            pltpu.VMEM(gradients.shape, bf16),
            roots,
            roots,
            message,
            message,
            message,
            by_step,
            by_step,
            message,
            arrivals,
            arrivals,
            tiles,
            gathered,
            gathered,
            tiles,
            tiles,
            gathered,
            gathered,
            tiles,
            diagonals,
            one_per_device,
            one_per_device,
            pltpu.VMEM((2, holders, 1, TILE_COLS), f32),
            diagonals,
            pltpu.VMEM((2, width, width), bf16),
            pltpu.VMEM((shards, 1, TILE_COLS), f32),
            pltpu.VMEM((holders, 1, TILE_COLS), f32),
            dma,
            dma,
            dma,
            dma,
            dma((4,)),
            dma((4,)),
            dma((4,)),
            dma((4,)),
            dma((CHUNKS,)),
            dma((CHUNKS,)),
            dma((CHUNKS,)),
            dma((CHUNKS,)),
            dma((7,)),
            dma((CHUNKS + 4,)),
        ],
        compiler_params=pltpu.CompilerParams(
            collective_id=0, has_side_effects=True, vmem_limit_bytes=VMEM_BYTES
        ),
    )(owners.reshape(1, blocks), gradients, left_roots, right_roots, left_stats, right_stats)
    parts = sum(out.shape[0] for out in outs)
    return pl.pallas_call(
        functools.partial(hand_over, len(outs)),
        name="hand_over",
        out_shape=outs,
        in_specs=[hbm] * 3,
        out_specs=(hbm,) * 3,
        scratch_shapes=[pltpu.VMEM(out.shape, out.dtype) for out in outs]
        + [dma((parts,)), dma((parts,))],
        compiler_params=pltpu.CompilerParams(vmem_limit_bytes=VMEM_BYTES),
    )(*results)


def solution(mesh):
    in_specs = (
        P(None, "tensor", "dp", None),
        P("tensor"),
        P(("dp", "tensor"), None, None),
        P(("dp", "tensor"), None, None),
        P(("dp", "tensor"), None, None),
        P(("dp", "tensor"), None, None),
    )
    out_specs = (
        P(None, "tensor", "dp", None),
        P(("dp", "tensor"), None, None),
        P(("dp", "tensor"), None, None),
    )
    return jax.shard_map(
        shards_step, mesh=mesh, in_specs=in_specs, out_specs=out_specs, check_vma=False
    )
```

```python
import functools

import jax
import jax.numpy as jnp
from jax import lax
from jax.experimental import pallas as pl
from jax.experimental.pallas import tpu as pltpu
from jax.sharding import PartitionSpec as P

SECOND_MOMENT = 0.95
CLIP_EPSILON = 1e-06
GRAFT_EPSILON = 1e-06
MESH = pl.DeviceIdType.MESH

CHUNKS = 2
VMEM_BYTES = 56 << 20
TILE_ROWS, TILE_COLS = 16, 128


def routes(owner_row):
    count = owner_row.shape[1]
    down = lax.broadcasted_iota(jnp.int32, (count, count), 0)
    across = lax.broadcasted_iota(jnp.int32, (count, count), 1)

    def along(mask, value, axis):
        return jnp.sum(jnp.where(mask, value, 0), axis=axis, keepdims=True)

    def column(row):
        return along(down == across, row, 1)

    def row(col):
        return along(down == across, col, 0)

    slot = along((column(owner_row) == owner_row) & (down < across), 1, 0)
    owned = owner_row == down
    load = along(owned, 1, 1)
    load_row = row(load)
    first_block = along(owned & (slot == 0), across, 1)
    second_block = along(owned & (slot == 1), across, 1)
    empty_rank = along((across < down) & (load_row == 0), 1, 1)
    second_rank = along((down < across) & (load > 1), 1, 0)
    match = (empty_rank == second_rank) & (load == 0) & (load_row > 1)
    helped = along(match, across, 1)
    helper = along(match, down, 0)
    helped_block = along(match, row(second_block), 1)
    block_of = jnp.where(load > 0, first_block, helped_block)
    device_of = along(block_of == across, down, 0)
    tables = (row(block_of), device_of, row(helped), helper)
    return tuple(jnp.minimum(table, count - 1) for table in tables) + (load_row,)


def kernel(
    sizes,
    owners_hbm,
    x_hbm,
    left_hbm,
    right_hbm,
    left_old_hbm,
    right_old_hbm,
    y_hbm,
    left_new_hbm,
    right_new_hbm,
    y_ref,
    left_new,
    right_new,
    left_old,
    right_old,
    owners_ref,
    table_ref,
    table,
    x_ref,
    left_roots,
    right_roots,
    byblock,
    stage,
    land,
    grads,
    outs,
    back_stage,
    back_first,
    back_second,
    roots_a,
    roots_b,
    roots_c,
    roots_d,
    grams_a,
    grams_b,
    grams_c,
    grams_d,
    diag_a,
    diag_b_roots,
    diag_b_grams,
    diag_c,
    diag_d,
    root_use,
    sums_y,
    sums_dp,
    send_y,
    recv_y,
    send_dp,
    recv_dp,
    send_tile,
    recv_tile,
    send_diag,
    recv_diag,
    send_go,
    recv_go,
    send_back,
    recv_back,
    load_sem,
    store_sem,
):
    steps, holders, shards, piece, width, total_count = sizes
    back = (back_first, back_second)
    chunk_steps = steps // CHUNKS
    rows = piece * chunk_steps
    group = width // rows
    groups = holders // group
    span = group * piece
    me = lax.axis_index("dp")
    shard = lax.axis_index("tensor")

    plane = holders // 8

    def peer(k):
        i = k - 1
        far = i < 7 * plane
        up = jnp.where(far, i % 7 + 1, 0)
        along = jnp.where(far, i // 7, i - 7 * plane + 1)
        return (me // plane + up) % 8 * plane + (me + along) % plane

    barrier = pltpu.get_barrier_semaphore()

    def greet(k, carry):
        pl.semaphore_signal(barrier, inc=1, device_id=(peer(k), shard), device_id_type=MESH)
        return carry

    def greet_shard(k, carry):
        pl.semaphore_signal(
            barrier, inc=1, device_id=(me, lax.rem(shard + k, shards)), device_id_type=MESH
        )
        return carry

    lax.fori_loop(1, shards, greet_shard, 0)
    lax.fori_loop(1, holders, greet, 0)

    loads = [
        pltpu.make_async_copy(source, target, load_sem.at[i])
        for i, (source, target) in enumerate(
            (
                (left_hbm, left_roots),
                (right_hbm, right_roots),
                (owners_hbm, owners_ref),
                (x_hbm, x_ref),
                (left_old_hbm, left_old),
                (right_old_hbm, right_old),
            )
        )
    ]
    for load in loads:
        load.start()

    out_index = lax.broadcasted_iota(jnp.int32, (width, width), 0)
    in_index = lax.broadcasted_iota(jnp.int32, (width, width), 1)

    def by_device(index):
        step, rest = index // span, index % span
        return (rest // piece) * rows + step * piece + rest % piece

    apart = (out_index == by_device(in_index)).astype(jnp.bfloat16)
    together = (by_device(out_index) == in_index).astype(jnp.bfloat16)

    def permute(matrix, values):
        return jnp.dot(matrix, values, preferred_element_type=jnp.float32).astype(jnp.bfloat16)

    def split_by_device(part):
        return jnp.dot(
            apart, part.reshape(width, width), preferred_element_type=jnp.float32
        ).reshape(group, rows, width)

    middle = width // 2
    quarter = middle // TILE_ROWS
    half = 2 * quarter
    count = 2 * half
    diag_b = (diag_b_roots, diag_b_grams)
    down = lax.broadcasted_iota(jnp.int32, (middle, middle), 0)
    across = lax.broadcasted_iota(jnp.int32, (middle, middle), 1)

    def pack(matrix, target, base):
        upper_left = matrix[:middle, :middle].astype(jnp.float32)
        lower_right = matrix[middle:, middle:].astype(jnp.float32)
        mixed = jnp.where(down >= across, upper_left, lower_right).astype(jnp.bfloat16)
        below = matrix[middle:, :middle].astype(jnp.bfloat16)
        target[base : base + quarter] = below.reshape(quarter, TILE_ROWS, middle)
        target[base + quarter : base + half] = mixed.reshape(quarter, TILE_ROWS, middle)
        return jnp.sum(jnp.where(down == across, lower_right, 0.0), axis=0, keepdims=True)

    def pack_pair(left, right, target, kind):
        diag_a[kind, 0] = pack(left, target, 0)
        diag_a[kind, 1] = pack(right, target, half)

    def unpack(source, side, kind):
        base = side * half
        below = source[base : base + quarter].reshape(middle, middle).astype(jnp.float32)
        mixed = source[base + quarter : base + half].reshape(middle, middle).astype(jnp.float32)
        diagonal = diag_d[kind, side]
        turned = mixed.T
        upper_left = jnp.where(down >= across, mixed, turned)
        lower_right = jnp.where(
            down < across, mixed, jnp.where(down > across, turned, diagonal)
        )
        return jnp.concatenate(
            [
                jnp.concatenate([upper_left, below.T], axis=1),
                jnp.concatenate([below, lower_right], axis=1),
            ],
            axis=0,
        )

    carries = lax.rem(me, 2) == 0
    mine = me // 2
    homes = (1, holders // 2 + 1)
    holds = (me == homes[0]) | (me == homes[1])
    my_side = jnp.where(me == homes[1], 1, 0)

    loads[0].wait()
    loads[1].wait()
    pack_pair(left_roots[1], right_roots[1], roots_a, 0)
    loads[2].wait()
    table_ref[...] = jnp.zeros_like(table_ref)
    for i, values in enumerate(routes(owners_ref[...])):
        table_ref[i : i + 1, :holders] = values
    table_copy = pltpu.make_async_copy(table_ref, table, load_sem.at[6])
    table_copy.start()
    loads[3].wait()

    lane = lax.broadcasted_iota(jnp.int32, (rows, TILE_COLS), 1)
    step_of = lax.broadcasted_iota(jnp.int32, (rows, TILE_COLS), 0) // piece
    local_row = jnp.zeros((1, TILE_COLS), jnp.float32)
    for c in range(CHUNKS):

        def prepare(g, total, c=c):
            part = x_ref[pl.ds(c * chunk_steps, chunk_steps), pl.ds(g * group, group)]
            done = split_by_device(part)
            byblock[c, pl.ds(g * group, group)] = done.astype(jnp.bfloat16)
            return total + jnp.sum(done * done, axis=0)

        squares = lax.fori_loop(0, groups, prepare, jnp.zeros((rows, width), jnp.float32))
        by_row = jnp.sum(squares, axis=1, keepdims=True)
        spot = lane == step_of + c * chunk_steps
        local_row = local_row + jnp.sum(jnp.where(spot, by_row, 0.0), axis=0, keepdims=True)
    sums_y[pl.ds(shard, 1)] = local_row[None]

    pl.semaphore_wait(barrier, holders - 1 + shards - 1)

    def copy(source, target, send, recv, device, t=None):
        return pltpu.make_async_remote_copy(
            src_ref=source,
            dst_ref=target,
            send_sem=send,
            recv_sem=recv,
            device_id=(device, shard if t is None else t),
            device_id_type=MESH,
        )

    def wait_bytes(ref, count, semaphore):
        part = ref.at[pl.ds(0, count)]
        pltpu.make_async_copy(part, part, semaphore).wait()

    def send_shard(k, carry):
        t = lax.rem(shard + k, shards)
        copy(sums_y.at[shard], sums_y.at[shard], send_y, recv_y, me, t).start()
        return carry

    lax.fori_loop(1, shards, send_shard, 0)

    def spread_tiles(source, target, which):
        def one(i, carry):
            chips = plane // 2
            far = i < 7 * chips
            up = jnp.where(far, i % 7 + 1, 0)
            along = jnp.where(far, i // 7, i - 7 * chips)
            chip = (me // plane + up) % 8 * chips + (me // 2 + along) % chips
            tile, d = chip, 2 * chip

            @pl.when(d != me)
            def _():
                copy(
                    source.at[tile], target.at[me], send_tile.at[which], recv_tile.at[which], d
                ).start()

            return carry

        lax.fori_loop(0, count, one, 0)

        @pl.when(carries)
        def _():
            target[me] = source[mine]

        kind = which // 2
        for side, d in enumerate(homes):

            @pl.when(me != d)
            def _(side=side, d=d):
                copy(
                    diag_a.at[kind, side],
                    diag_b[kind].at[me],
                    send_diag.at[which],
                    recv_diag.at[which],
                    d,
                ).start()

            @pl.when(me == d)
            def _(side=side):
                diag_b[kind][me] = diag_a[kind, side]

    def pass_tiles(source, staged, target, which, row):
        @pl.when(carries)
        def _():
            wait_bytes(source, holders - 1, recv_tile.at[which - 1])

            def one(k, carry):
                d = peer(k)
                staged[d] = source[table[row, d]]
                copy(
                    staged.at[d], target.at[mine], send_tile.at[which], recv_tile.at[which], d
                ).start()
                return carry

            lax.fori_loop(1, holders, one, 0)
            target[mine] = source[table[row, me]]

        @pl.when(holds)
        def _():
            kind = which // 2
            rows_in = diag_b[kind]
            wait_bytes(rows_in, holders - 1, recv_diag.at[which - 1])

            def one(k, carry):
                d = peer(k)
                diag_c[kind, d] = rows_in[table[row, d]]
                copy(
                    diag_c.at[kind, d],
                    diag_d.at[kind, my_side],
                    send_diag.at[which],
                    recv_diag.at[which],
                    d,
                ).start()
                return carry

            lax.fori_loop(1, holders, one, 0)
            diag_d[kind, my_side] = rows_in[table[row, me]]

    def wait_tiles(tiles, semaphore, diagonal_semaphore):
        @pl.when(carries)
        def _():
            wait_bytes(tiles, count - 1, semaphore)

        @pl.when(jnp.logical_not(carries))
        def _():
            wait_bytes(tiles, count, semaphore)

        @pl.when(holds)
        def _():
            wait_bytes(diag_d.at[0], 1, diagonal_semaphore)

        @pl.when(jnp.logical_not(holds))
        def _():
            wait_bytes(diag_d.at[0], 2, diagonal_semaphore)

    spread_tiles(roots_a, roots_b, 0)

    table_copy.wait()

    def send_gradients(c):
        def one(k, carry):
            d = peer(k)
            stage[c, d] = byblock[c, table[0, d]]
            copy(stage.at[c, d], land.at[c, me], send_go.at[c], recv_go.at[c], d).start()
            return carry

        lax.fori_loop(1, holders, one, 0)
        land[c, me] = byblock[c, table[0, me]]

    send_gradients(0)

    wait_bytes(sums_y, shards - 1, recv_y)
    shard_row = sums_y[0]
    for t in range(1, shards):
        shard_row = shard_row + sums_y[t]
    sums_dp[pl.ds(me, 1)] = shard_row[None]

    def send_sums(k, carry):
        d = peer(k)
        copy(sums_dp.at[me], sums_dp.at[me], send_dp, recv_dp, d).start()
        return carry

    lax.fori_loop(1, holders, send_sums, 0)

    pass_tiles(roots_b, roots_c, roots_d, 1, 2)

    for c in range(1, CHUNKS):
        send_gradients(c)

    wait_bytes(sums_dp, holders - 1, recv_dp)
    totals = jnp.sum(sums_dp[...], axis=0)
    clip_row = jnp.minimum(1.0, 1.0 / jnp.sqrt(totals / total_count + CLIP_EPSILON))

    def clip_of(s):
        return jnp.sum(jnp.where(lane[:1] == s, clip_row, 0.0), axis=1, keepdims=True)

    load = table[4, me]

    def gather_steps(c):
        wait_bytes(land.at[c], holders - 1, recv_go.at[c])

        def one(g, carry):
            values = land[c, pl.ds(g * group, group)].reshape(width, width)
            done = permute(together, values).reshape(chunk_steps, span, width)
            grads[pl.ds(c * chunk_steps, chunk_steps), pl.ds(g * span, span), :] = done
            return carry

        lax.fori_loop(0, groups, one, 0)

    def directions(c):
        def one(s, carry):
            gradient = grads[s]
            wide = gradient.astype(jnp.float32)
            square = jnp.sum(wide * wide, axis=(0, 1), keepdims=True)
            left_part = jnp.dot(
                root_use[0], gradient, preferred_element_type=jnp.float32
            ).astype(jnp.bfloat16)
            direction = jnp.dot(left_part, root_use[1], preferred_element_type=jnp.float32)
            direction_square = jnp.sum(direction * direction, axis=(0, 1), keepdims=True)
            area = float(width * width)
            ratio = (
                clip_of(s)
                * jnp.sqrt(square / area)
                / jnp.sqrt(direction_square / area + GRAFT_EPSILON)
            )
            outs[s] = (ratio * direction).astype(jnp.bfloat16)
            return carry

        lax.fori_loop(c * chunk_steps, (c + 1) * chunk_steps, one, 0)

        def sort(g, carry):
            part = outs[pl.ds(c * chunk_steps, chunk_steps), pl.ds(g * span, span), :]
            back_stage[c, pl.ds(g * group, group)] = split_by_device(part).astype(jnp.bfloat16)
            return carry

        lax.fori_loop(0, groups, sort, 0)

        def send(k, carry):
            d = peer(k)
            copy(
                back_stage.at[c, d], back[c].at[me], send_back.at[c], recv_back.at[c], d
            ).start()
            return carry

        lax.fori_loop(1, holders // 2, send, 0)
        if c == CHUNKS - 1:
            pass_tiles(grams_b, grams_c, grams_d, 3, 3)
        lax.fori_loop(holders // 2, holders, send, 0)
        back[c][me] = back_stage[c, me]

    left_new[0] = jnp.zeros((width, width), jnp.float32)
    right_new[0] = jnp.zeros((width, width), jnp.float32)

    def add_gram(s, carry):
        gradient = grads[s]
        clip = clip_of(s)
        weight = (1.0 - SECOND_MOMENT) * clip * clip / width
        left = lax.dot_general(
            gradient, gradient, (((1,), (1,)), ((), ())), preferred_element_type=jnp.float32
        )
        right = lax.dot_general(
            gradient, gradient, (((0,), (0,)), ((), ())), preferred_element_type=jnp.float32
        )
        left_new[0] = SECOND_MOMENT * left_new[0] + weight * left
        right_new[0] = SECOND_MOMENT * right_new[0] + weight * right
        return carry

    def add_grams(c):
        lax.fori_loop(c * chunk_steps, (c + 1) * chunk_steps, add_gram, 0)

    gather_steps(0)
    wait_tiles(roots_d, recv_tile.at[1], recv_diag.at[1])
    for side, own in enumerate((left_roots, right_roots)):
        sent = unpack(roots_d, side, 0).astype(jnp.bfloat16)
        root_use[side] = jnp.where(load > 0, own[0], sent)
    for c in range(CHUNKS - 1):
        directions(c)
        add_grams(c)
        gather_steps(c + 1)
    add_grams(CHUNKS - 1)

    pack_pair(left_new[0], right_new[0], grams_a, 1)
    spread_tiles(grams_a, grams_b, 2)
    directions(CHUNKS - 1)

    kept = SECOND_MOMENT**steps
    stores = []

    def store(source, target):
        done = pltpu.make_async_copy(source, target, store_sem.at[len(stores)])
        done.start()
        stores.append(done)

    sides = ((left_old, left_new, left_new_hbm), (right_old, right_new, right_new_hbm))
    for side, (old, new, target) in enumerate(sides):
        loads[4 + side].wait()
        new[0] = jnp.where(load > 0, kept * old[0] + new[0], old[0])
        store(new.at[0], target.at[0])

    def finish(c):
        wait_bytes(back[c], holders - 1, recv_back.at[c])

        def one(g, carry):
            values = jnp.concatenate(
                [back[c][table[1, g * group + i]] for i in range(group)], axis=0
            )
            done = permute(together, values).reshape(chunk_steps, group, piece, width)
            y_ref[pl.ds(c * chunk_steps, chunk_steps), pl.ds(g * group, group)] = done
            return carry

        lax.fori_loop(0, groups, one, 0)
        part = pl.ds(c * chunk_steps, chunk_steps)
        store(y_ref.at[part], y_hbm.at[part])

    for c in range(CHUNKS):
        finish(c)

    wait_tiles(grams_d, recv_tile.at[3], recv_diag.at[3])
    for side, (old, new, target) in enumerate(sides):
        new[1] = jnp.where(load > 1, kept * old[1] + unpack(grams_d, side, 1), old[1])
        store(new.at[1], target.at[1])

    wait_bytes(sums_y, shards - 1, send_y)
    wait_bytes(sums_dp, holders - 1, send_dp)
    for which in (0, 2):
        wait_tiles(roots_a, send_tile.at[which], send_diag.at[which])

        @pl.when(carries)
        def _():
            wait_bytes(roots_b, holders - 1, send_tile.at[which + 1])

        @pl.when(holds)
        def _():
            wait_bytes(diag_b_roots, holders - 1, send_diag.at[which + 1])

    for c in range(CHUNKS):
        wait_bytes(stage.at[c], holders - 1, send_go.at[c])
        wait_bytes(back_stage.at[c], holders - 1, send_back.at[c])
    for done in stores:
        done.wait()


def hand_over(count, *refs):
    inputs, outputs, rooms = refs[:count], refs[count : 2 * count], refs[2 * count : 3 * count]
    load_sem, store_sem = refs[3 * count :]
    parts = [(k, i) for k in range(count) for i in range(inputs[k].shape[0])]
    loads, stores = [], []
    for n, (k, i) in enumerate(parts):
        loads.append(pltpu.make_async_copy(inputs[k].at[i], rooms[k].at[i], load_sem.at[n]))
        stores.append(pltpu.make_async_copy(rooms[k].at[i], outputs[k].at[i], store_sem.at[n]))
    for load in loads:
        load.start()
    for load, store in zip(loads, stores):
        load.wait()
        store.start()
    for store in stores:
        store.wait()


def shards_step(gradients, owners, left_stats, right_stats, left_roots, right_roots):
    steps, blocks, piece, width = gradients.shape
    holders = lax.axis_size("dp")
    shards = lax.axis_size("tensor")
    rows = piece * (steps // CHUNKS)
    total_count = float(holders * shards * blocks * piece * width)
    bf16, f32 = jnp.bfloat16, jnp.float32
    message = pltpu.VMEM((CHUNKS, blocks, rows, width), bf16)
    arrivals = pltpu.VMEM((blocks, rows, width), bf16)
    by_step = pltpu.VMEM((steps, width, width), bf16)
    pieces = 2 * width // TILE_ROWS
    tiles = pltpu.VMEM((pieces, TILE_ROWS, TILE_COLS), bf16)
    gathered = pltpu.VMEM((holders, TILE_ROWS, TILE_COLS), bf16)
    diagonals = pltpu.VMEM((2, 2, 1, TILE_COLS), f32)
    one_per_device = pltpu.VMEM((holders, 1, TILE_COLS), f32)
    roots = pltpu.VMEM(left_roots.shape, bf16)
    dma = pltpu.SemaphoreType.DMA
    hbm = pl.BlockSpec(memory_space=pl.ANY)
    sizes = (steps, holders, shards, piece, width, total_count)
    outs = (
        jax.ShapeDtypeStruct(gradients.shape, bf16),
        jax.ShapeDtypeStruct(left_stats.shape, f32),
        jax.ShapeDtypeStruct(right_stats.shape, f32),
    )
    stats = pltpu.VMEM(left_stats.shape, f32)
    results = pl.pallas_call(
        functools.partial(kernel, sizes),
        name="shampoo",
        out_shape=outs,
        in_specs=[hbm] * 6,
        out_specs=(hbm,) * 3,
        scratch_shapes=[
            pltpu.VMEM(gradients.shape, bf16),
            stats,
            stats,
            stats,
            stats,
            pltpu.VMEM((1, blocks), jnp.int32),
            pltpu.VMEM((8, TILE_COLS), jnp.int32),
            pltpu.SMEM((8, TILE_COLS), jnp.int32),
            pltpu.VMEM(gradients.shape, bf16),
            roots,
            roots,
            message,
            message,
            message,
            by_step,
            by_step,
            message,
            arrivals,
            arrivals,
            tiles,
            gathered,
            gathered,
            tiles,
            tiles,
            gathered,
            gathered,
            tiles,
            diagonals,
            one_per_device,
            one_per_device,
            pltpu.VMEM((2, holders, 1, TILE_COLS), f32),
            diagonals,
            pltpu.VMEM((2, width, width), bf16),
            pltpu.VMEM((shards, 1, TILE_COLS), f32),
            pltpu.VMEM((holders, 1, TILE_COLS), f32),
            dma,
            dma,
            dma,
            dma,
            dma((4,)),
            dma((4,)),
            dma((4,)),
            dma((4,)),
            dma((CHUNKS,)),
            dma((CHUNKS,)),
            dma((CHUNKS,)),
            dma((CHUNKS,)),
            dma((7,)),
            dma((CHUNKS + 4,)),
        ],
        compiler_params=pltpu.CompilerParams(
            collective_id=0, has_side_effects=True, vmem_limit_bytes=VMEM_BYTES
        ),
    )(owners.reshape(1, blocks), gradients, left_roots, right_roots, left_stats, right_stats)
    parts = sum(out.shape[0] for out in outs)
    return pl.pallas_call(
        functools.partial(hand_over, len(outs)),
        name="hand_over",
        out_shape=outs,
        in_specs=[hbm] * 3,
        out_specs=(hbm,) * 3,
        scratch_shapes=[pltpu.VMEM(out.shape, out.dtype) for out in outs]
        + [dma((parts,)), dma((parts,))],
        compiler_params=pltpu.CompilerParams(vmem_limit_bytes=VMEM_BYTES),
    )(*results)


def solution(mesh):
    in_specs = (
        P(None, "tensor", "dp", None),
        P("tensor"),
        P(("dp", "tensor"), None, None),
        P(("dp", "tensor"), None, None),
        P(("dp", "tensor"), None, None),
        P(("dp", "tensor"), None, None),
    )
    out_specs = (
        P(None, "tensor", "dp", None),
        P(("dp", "tensor"), None, None),
        P(("dp", "tensor"), None, None),
    )
    return jax.shard_map(
        shards_step, mesh=mesh, in_specs=in_specs, out_specs=out_specs, check_vma=False
    )
```

```python
import functools

import jax
import jax.numpy as jnp
from jax import lax
from jax.experimental import pallas as pl
from jax.experimental.pallas import tpu as pltpu
from jax.sharding import PartitionSpec as P

SECOND_MOMENT = 0.95
CLIP_EPSILON = 1e-06
GRAFT_EPSILON = 1e-06
MESH = pl.DeviceIdType.MESH

CHUNKS = 2
VMEM_BYTES = 56 << 20
TILE_ROWS, TILE_COLS = 16, 128


def routes(owner_row):
    count = owner_row.shape[1]
    down = lax.broadcasted_iota(jnp.int32, (count, count), 0)
    across = lax.broadcasted_iota(jnp.int32, (count, count), 1)

    def along(mask, value, axis):
        return jnp.sum(jnp.where(mask, value, 0), axis=axis, keepdims=True)

    def column(row):
        return along(down == across, row, 1)

    def row(col):
        return along(down == across, col, 0)

    slot = along((column(owner_row) == owner_row) & (down < across), 1, 0)
    owned = owner_row == down
    load = along(owned, 1, 1)
    load_row = row(load)
    first_block = along(owned & (slot == 0), across, 1)
    second_block = along(owned & (slot == 1), across, 1)
    empty_rank = along((across < down) & (load_row == 0), 1, 1)
    second_rank = along((down < across) & (load > 1), 1, 0)
    match = (empty_rank == second_rank) & (load == 0) & (load_row > 1)
    helped = along(match, across, 1)
    helper = along(match, down, 0)
    helped_block = along(match, row(second_block), 1)
    block_of = jnp.where(load > 0, first_block, helped_block)
    device_of = along(block_of == across, down, 0)
    tables = (row(block_of), device_of, row(helped), helper)
    return tuple(jnp.minimum(table, count - 1) for table in tables) + (load_row,)


def kernel(
    sizes,
    owners_hbm,
    x_hbm,
    left_hbm,
    right_hbm,
    left_old_hbm,
    right_old_hbm,
    y_hbm,
    left_new_hbm,
    right_new_hbm,
    y_ref,
    left_new,
    right_new,
    left_old,
    right_old,
    owners_ref,
    table_ref,
    table,
    x_ref,
    left_roots,
    right_roots,
    byblock,
    stage,
    land,
    grads,
    outs,
    back_stage,
    back_first,
    back_second,
    roots_a,
    roots_b,
    roots_c,
    roots_d,
    grams_a,
    grams_b,
    grams_c,
    grams_d,
    diag_a,
    diag_b_roots,
    diag_b_grams,
    diag_c,
    diag_d,
    root_use,
    sums_y,
    sums_dp,
    send_y,
    recv_y,
    send_dp,
    recv_dp,
    send_tile,
    recv_tile,
    send_diag,
    recv_diag,
    send_go,
    recv_go,
    send_back,
    recv_back,
    load_sem,
    store_sem,
):
    steps, holders, shards, piece, width, total_count = sizes
    back = (back_first, back_second)
    chunk_steps = steps // CHUNKS
    rows = piece * chunk_steps
    group = width // rows
    groups = holders // group
    span = group * piece
    me = lax.axis_index("dp")
    shard = lax.axis_index("tensor")

    plane = holders // 8

    def peer(k):
        i = k - 1
        far = i < 7 * plane
        up = jnp.where(far, i % 7 + 1, 0)
        along = jnp.where(far, i // 7, i - 7 * plane + 1)
        return (me // plane + up) % 8 * plane + (me + along) % plane

    barrier = pltpu.get_barrier_semaphore()

    def greet(k, carry):
        pl.semaphore_signal(barrier, inc=1, device_id=(peer(k), shard), device_id_type=MESH)
        return carry

    def greet_shard(k, carry):
        pl.semaphore_signal(
            barrier, inc=1, device_id=(me, lax.rem(shard + k, shards)), device_id_type=MESH
        )
        return carry

    lax.fori_loop(1, shards, greet_shard, 0)
    lax.fori_loop(1, holders, greet, 0)

    loads = [
        pltpu.make_async_copy(source, target, load_sem.at[i])
        for i, (source, target) in enumerate(
            (
                (left_hbm, left_roots),
                (right_hbm, right_roots),
                (owners_hbm, owners_ref),
                (x_hbm, x_ref),
                (left_old_hbm, left_old),
                (right_old_hbm, right_old),
            )
        )
    ]
    for load in loads:
        load.start()

    out_index = lax.broadcasted_iota(jnp.int32, (width, width), 0)
    in_index = lax.broadcasted_iota(jnp.int32, (width, width), 1)

    def by_device(index):
        step, rest = index // span, index % span
        return (rest // piece) * rows + step * piece + rest % piece

    apart = (out_index == by_device(in_index)).astype(jnp.bfloat16)
    together = (by_device(out_index) == in_index).astype(jnp.bfloat16)

    def permute(matrix, values):
        return jnp.dot(matrix, values, preferred_element_type=jnp.float32).astype(jnp.bfloat16)

    def split_by_device(part):
        return jnp.dot(
            apart, part.reshape(width, width), preferred_element_type=jnp.float32
        ).reshape(group, rows, width)

    middle = width // 2
    quarter = middle // TILE_ROWS
    half = 2 * quarter
    count = 2 * half
    diag_b = (diag_b_roots, diag_b_grams)
    down = lax.broadcasted_iota(jnp.int32, (middle, middle), 0)
    across = lax.broadcasted_iota(jnp.int32, (middle, middle), 1)

    def pack(matrix, target, base):
        upper_left = matrix[:middle, :middle].astype(jnp.float32)
        lower_right = matrix[middle:, middle:].astype(jnp.float32)
        mixed = jnp.where(down >= across, upper_left, lower_right).astype(jnp.bfloat16)
        below = matrix[middle:, :middle].astype(jnp.bfloat16)
        target[base : base + quarter] = below.reshape(quarter, TILE_ROWS, middle)
        target[base + quarter : base + half] = mixed.reshape(quarter, TILE_ROWS, middle)
        return jnp.sum(jnp.where(down == across, lower_right, 0.0), axis=0, keepdims=True)

    def pack_pair(left, right, target, kind):
        diag_a[kind, 0] = pack(left, target, 0)
        diag_a[kind, 1] = pack(right, target, half)

    def unpack(source, side, kind):
        base = side * half
        below = source[base : base + quarter].reshape(middle, middle).astype(jnp.float32)
        mixed = source[base + quarter : base + half].reshape(middle, middle).astype(jnp.float32)
        diagonal = diag_d[kind, side]
        turned = mixed.T
        upper_left = jnp.where(down >= across, mixed, turned)
        lower_right = jnp.where(
            down < across, mixed, jnp.where(down > across, turned, diagonal)
        )
        return jnp.concatenate(
            [
                jnp.concatenate([upper_left, below.T], axis=1),
                jnp.concatenate([below, lower_right], axis=1),
            ],
            axis=0,
        )

    carries = lax.rem(me, 2) == lax.rem(me // 2, 2)
    mine = me // 2
    homes = (1, holders // 2 + 1)
    holds = (me == homes[0]) | (me == homes[1])
    my_side = jnp.where(me == homes[1], 1, 0)

    loads[0].wait()
    loads[1].wait()
    pack_pair(left_roots[1], right_roots[1], roots_a, 0)
    loads[2].wait()
    table_ref[...] = jnp.zeros_like(table_ref)
    for i, values in enumerate(routes(owners_ref[...])):
        table_ref[i : i + 1, :holders] = values
    table_copy = pltpu.make_async_copy(table_ref, table, load_sem.at[6])
    table_copy.start()
    loads[3].wait()

    lane = lax.broadcasted_iota(jnp.int32, (rows, TILE_COLS), 1)
    step_of = lax.broadcasted_iota(jnp.int32, (rows, TILE_COLS), 0) // piece
    local_row = jnp.zeros((1, TILE_COLS), jnp.float32)
    for c in range(CHUNKS):

        def prepare(g, total, c=c):
            part = x_ref[pl.ds(c * chunk_steps, chunk_steps), pl.ds(g * group, group)]
            done = split_by_device(part)
            byblock[c, pl.ds(g * group, group)] = done.astype(jnp.bfloat16)
            return total + jnp.sum(done * done, axis=0)

        squares = lax.fori_loop(0, groups, prepare, jnp.zeros((rows, width), jnp.float32))
        by_row = jnp.sum(squares, axis=1, keepdims=True)
        spot = lane == step_of + c * chunk_steps
        local_row = local_row + jnp.sum(jnp.where(spot, by_row, 0.0), axis=0, keepdims=True)
    sums_y[pl.ds(shard, 1)] = local_row[None]

    pl.semaphore_wait(barrier, holders - 1 + shards - 1)

    def copy(source, target, send, recv, device, t=None):
        return pltpu.make_async_remote_copy(
            src_ref=source,
            dst_ref=target,
            send_sem=send,
            recv_sem=recv,
            device_id=(device, shard if t is None else t),
            device_id_type=MESH,
        )

    def wait_bytes(ref, count, semaphore):
        part = ref.at[pl.ds(0, count)]
        pltpu.make_async_copy(part, part, semaphore).wait()

    def send_shard(k, carry):
        t = lax.rem(shard + k, shards)
        copy(sums_y.at[shard], sums_y.at[shard], send_y, recv_y, me, t).start()
        return carry

    lax.fori_loop(1, shards, send_shard, 0)

    def spread_tiles(source, target, which):
        def one(i, carry):
            chips = plane // 2
            far = i < 7 * chips
            up = jnp.where(far, i % 7 + 1, 0)
            along = jnp.where(far, i // 7, i - 7 * chips)
            chip = (me // plane + up) % 8 * chips + (me // 2 + along) % chips
            tile, d = chip, 2 * chip + chip % 2

            @pl.when(d != me)
            def _():
                copy(
                    source.at[tile], target.at[me], send_tile.at[which], recv_tile.at[which], d
                ).start()

            return carry

        lax.fori_loop(0, count, one, 0)

        @pl.when(carries)
        def _():
            target[me] = source[mine]

        kind = which // 2
        for side, d in enumerate(homes):

            @pl.when(me != d)
            def _(side=side, d=d):
                copy(
                    diag_a.at[kind, side],
                    diag_b[kind].at[me],
                    send_diag.at[which],
                    recv_diag.at[which],
                    d,
                ).start()

            @pl.when(me == d)
            def _(side=side):
                diag_b[kind][me] = diag_a[kind, side]

    def pass_tiles(source, staged, target, which, row):
        @pl.when(carries)
        def _():
            wait_bytes(source, holders - 1, recv_tile.at[which - 1])

            def one(k, carry):
                d = peer(k)
                staged[d] = source[table[row, d]]
                copy(
                    staged.at[d], target.at[mine], send_tile.at[which], recv_tile.at[which], d
                ).start()
                return carry

            lax.fori_loop(1, holders, one, 0)
            target[mine] = source[table[row, me]]

        @pl.when(holds)
        def _():
            kind = which // 2
            rows_in = diag_b[kind]
            wait_bytes(rows_in, holders - 1, recv_diag.at[which - 1])

            def one(k, carry):
                d = peer(k)
                diag_c[kind, d] = rows_in[table[row, d]]
                copy(
                    diag_c.at[kind, d],
                    diag_d.at[kind, my_side],
                    send_diag.at[which],
                    recv_diag.at[which],
                    d,
                ).start()
                return carry

            lax.fori_loop(1, holders, one, 0)
            diag_d[kind, my_side] = rows_in[table[row, me]]

    def wait_tiles(tiles, semaphore, diagonal_semaphore):
        @pl.when(carries)
        def _():
            wait_bytes(tiles, count - 1, semaphore)

        @pl.when(jnp.logical_not(carries))
        def _():
            wait_bytes(tiles, count, semaphore)

        @pl.when(holds)
        def _():
            wait_bytes(diag_d.at[0], 1, diagonal_semaphore)

        @pl.when(jnp.logical_not(holds))
        def _():
            wait_bytes(diag_d.at[0], 2, diagonal_semaphore)

    spread_tiles(roots_a, roots_b, 0)

    table_copy.wait()

    def send_gradients(c):
        def one(k, carry):
            d = peer(k)
            stage[c, d] = byblock[c, table[0, d]]
            copy(stage.at[c, d], land.at[c, me], send_go.at[c], recv_go.at[c], d).start()
            return carry

        lax.fori_loop(1, holders, one, 0)
        land[c, me] = byblock[c, table[0, me]]

    send_gradients(0)

    wait_bytes(sums_y, shards - 1, recv_y)
    shard_row = sums_y[0]
    for t in range(1, shards):
        shard_row = shard_row + sums_y[t]
    sums_dp[pl.ds(me, 1)] = shard_row[None]

    def send_sums(k, carry):
        d = peer(k)
        copy(sums_dp.at[me], sums_dp.at[me], send_dp, recv_dp, d).start()
        return carry

    lax.fori_loop(1, holders, send_sums, 0)

    pass_tiles(roots_b, roots_c, roots_d, 1, 2)

    for c in range(1, CHUNKS):
        send_gradients(c)

    wait_bytes(sums_dp, holders - 1, recv_dp)
    totals = jnp.sum(sums_dp[...], axis=0)
    clip_row = jnp.minimum(1.0, 1.0 / jnp.sqrt(totals / total_count + CLIP_EPSILON))

    def clip_of(s):
        return jnp.sum(jnp.where(lane[:1] == s, clip_row, 0.0), axis=1, keepdims=True)

    load = table[4, me]

    def gather_steps(c):
        wait_bytes(land.at[c], holders - 1, recv_go.at[c])

        def one(g, carry):
            values = land[c, pl.ds(g * group, group)].reshape(width, width)
            done = permute(together, values).reshape(chunk_steps, span, width)
            grads[pl.ds(c * chunk_steps, chunk_steps), pl.ds(g * span, span), :] = done
            return carry

        lax.fori_loop(0, groups, one, 0)

    def directions(c):
        def one(s, carry):
            gradient = grads[s]
            wide = gradient.astype(jnp.float32)
            square = jnp.sum(wide * wide, axis=(0, 1), keepdims=True)
            left_part = jnp.dot(
                root_use[0], gradient, preferred_element_type=jnp.float32
            ).astype(jnp.bfloat16)
            direction = jnp.dot(left_part, root_use[1], preferred_element_type=jnp.float32)
            direction_square = jnp.sum(direction * direction, axis=(0, 1), keepdims=True)
            area = float(width * width)
            ratio = (
                clip_of(s)
                * jnp.sqrt(square / area)
                / jnp.sqrt(direction_square / area + GRAFT_EPSILON)
            )
            outs[s] = (ratio * direction).astype(jnp.bfloat16)
            return carry

        lax.fori_loop(c * chunk_steps, (c + 1) * chunk_steps, one, 0)

        def sort(g, carry):
            part = outs[pl.ds(c * chunk_steps, chunk_steps), pl.ds(g * span, span), :]
            back_stage[c, pl.ds(g * group, group)] = split_by_device(part).astype(jnp.bfloat16)
            return carry

        lax.fori_loop(0, groups, sort, 0)

        def send(k, carry):
            d = peer(k)
            copy(
                back_stage.at[c, d], back[c].at[me], send_back.at[c], recv_back.at[c], d
            ).start()
            return carry

        lax.fori_loop(1, holders // 2, send, 0)
        if c == CHUNKS - 1:
            pass_tiles(grams_b, grams_c, grams_d, 3, 3)
        lax.fori_loop(holders // 2, holders, send, 0)
        back[c][me] = back_stage[c, me]

    left_new[0] = jnp.zeros((width, width), jnp.float32)
    right_new[0] = jnp.zeros((width, width), jnp.float32)

    def add_gram(s, carry):
        gradient = grads[s]
        clip = clip_of(s)
        weight = (1.0 - SECOND_MOMENT) * clip * clip / width
        left = lax.dot_general(
            gradient, gradient, (((1,), (1,)), ((), ())), preferred_element_type=jnp.float32
        )
        right = lax.dot_general(
            gradient, gradient, (((0,), (0,)), ((), ())), preferred_element_type=jnp.float32
        )
        left_new[0] = SECOND_MOMENT * left_new[0] + weight * left
        right_new[0] = SECOND_MOMENT * right_new[0] + weight * right
        return carry

    def add_grams(c):
        lax.fori_loop(c * chunk_steps, (c + 1) * chunk_steps, add_gram, 0)

    gather_steps(0)
    wait_tiles(roots_d, recv_tile.at[1], recv_diag.at[1])
    for side, own in enumerate((left_roots, right_roots)):
        sent = unpack(roots_d, side, 0).astype(jnp.bfloat16)
        root_use[side] = jnp.where(load > 0, own[0], sent)
    for c in range(CHUNKS - 1):
        directions(c)
        add_grams(c)
        gather_steps(c + 1)
    add_grams(CHUNKS - 1)

    pack_pair(left_new[0], right_new[0], grams_a, 1)
    spread_tiles(grams_a, grams_b, 2)
    directions(CHUNKS - 1)

    kept = SECOND_MOMENT**steps
    stores = []

    def store(source, target):
        done = pltpu.make_async_copy(source, target, store_sem.at[len(stores)])
        done.start()
        stores.append(done)

    sides = ((left_old, left_new, left_new_hbm), (right_old, right_new, right_new_hbm))
    for side, (old, new, target) in enumerate(sides):
        loads[4 + side].wait()
        new[0] = jnp.where(load > 0, kept * old[0] + new[0], old[0])
        store(new.at[0], target.at[0])

    def finish(c):
        wait_bytes(back[c], holders - 1, recv_back.at[c])

        def one(g, carry):
            values = jnp.concatenate(
                [back[c][table[1, g * group + i]] for i in range(group)], axis=0
            )
            done = permute(together, values).reshape(chunk_steps, group, piece, width)
            y_ref[pl.ds(c * chunk_steps, chunk_steps), pl.ds(g * group, group)] = done
            return carry

        lax.fori_loop(0, groups, one, 0)
        part = pl.ds(c * chunk_steps, chunk_steps)
        store(y_ref.at[part], y_hbm.at[part])

    for c in range(CHUNKS):
        finish(c)

    wait_tiles(grams_d, recv_tile.at[3], recv_diag.at[3])
    for side, (old, new, target) in enumerate(sides):
        new[1] = jnp.where(load > 1, kept * old[1] + unpack(grams_d, side, 1), old[1])
        store(new.at[1], target.at[1])

    wait_bytes(sums_y, shards - 1, send_y)
    wait_bytes(sums_dp, holders - 1, send_dp)
    for which in (0, 2):
        wait_tiles(roots_a, send_tile.at[which], send_diag.at[which])

        @pl.when(carries)
        def _():
            wait_bytes(roots_b, holders - 1, send_tile.at[which + 1])

        @pl.when(holds)
        def _():
            wait_bytes(diag_b_roots, holders - 1, send_diag.at[which + 1])

    for c in range(CHUNKS):
        wait_bytes(stage.at[c], holders - 1, send_go.at[c])
        wait_bytes(back_stage.at[c], holders - 1, send_back.at[c])
    for done in stores:
        done.wait()


def hand_over(count, *refs):
    inputs, outputs, rooms = refs[:count], refs[count : 2 * count], refs[2 * count : 3 * count]
    load_sem, store_sem = refs[3 * count :]
    parts = [(k, i) for k in range(count) for i in range(inputs[k].shape[0])]
    loads, stores = [], []
    for n, (k, i) in enumerate(parts):
        loads.append(pltpu.make_async_copy(inputs[k].at[i], rooms[k].at[i], load_sem.at[n]))
        stores.append(pltpu.make_async_copy(rooms[k].at[i], outputs[k].at[i], store_sem.at[n]))
    for load in loads:
        load.start()
    for load, store in zip(loads, stores):
        load.wait()
        store.start()
    for store in stores:
        store.wait()


def shards_step(gradients, owners, left_stats, right_stats, left_roots, right_roots):
    steps, blocks, piece, width = gradients.shape
    holders = lax.axis_size("dp")
    shards = lax.axis_size("tensor")
    rows = piece * (steps // CHUNKS)
    total_count = float(holders * shards * blocks * piece * width)
    bf16, f32 = jnp.bfloat16, jnp.float32
    message = pltpu.VMEM((CHUNKS, blocks, rows, width), bf16)
    arrivals = pltpu.VMEM((blocks, rows, width), bf16)
    by_step = pltpu.VMEM((steps, width, width), bf16)
    pieces = 2 * width // TILE_ROWS
    tiles = pltpu.VMEM((pieces, TILE_ROWS, TILE_COLS), bf16)
    gathered = pltpu.VMEM((holders, TILE_ROWS, TILE_COLS), bf16)
    diagonals = pltpu.VMEM((2, 2, 1, TILE_COLS), f32)
    one_per_device = pltpu.VMEM((holders, 1, TILE_COLS), f32)
    roots = pltpu.VMEM(left_roots.shape, bf16)
    dma = pltpu.SemaphoreType.DMA
    hbm = pl.BlockSpec(memory_space=pl.ANY)
    sizes = (steps, holders, shards, piece, width, total_count)
    outs = (
        jax.ShapeDtypeStruct(gradients.shape, bf16),
        jax.ShapeDtypeStruct(left_stats.shape, f32),
        jax.ShapeDtypeStruct(right_stats.shape, f32),
    )
    stats = pltpu.VMEM(left_stats.shape, f32)
    results = pl.pallas_call(
        functools.partial(kernel, sizes),
        name="shampoo",
        out_shape=outs,
        in_specs=[hbm] * 6,
        out_specs=(hbm,) * 3,
        scratch_shapes=[
            pltpu.VMEM(gradients.shape, bf16),
            stats,
            stats,
            stats,
            stats,
            pltpu.VMEM((1, blocks), jnp.int32),
            pltpu.VMEM((8, TILE_COLS), jnp.int32),
            pltpu.SMEM((8, TILE_COLS), jnp.int32),
            pltpu.VMEM(gradients.shape, bf16),
            roots,
            roots,
            message,
            message,
            message,
            by_step,
            by_step,
            message,
            arrivals,
            arrivals,
            tiles,
            gathered,
            gathered,
            tiles,
            tiles,
            gathered,
            gathered,
            tiles,
            diagonals,
            one_per_device,
            one_per_device,
            pltpu.VMEM((2, holders, 1, TILE_COLS), f32),
            diagonals,
            pltpu.VMEM((2, width, width), bf16),
            pltpu.VMEM((shards, 1, TILE_COLS), f32),
            pltpu.VMEM((holders, 1, TILE_COLS), f32),
            dma,
            dma,
            dma,
            dma,
            dma((4,)),
            dma((4,)),
            dma((4,)),
            dma((4,)),
            dma((CHUNKS,)),
            dma((CHUNKS,)),
            dma((CHUNKS,)),
            dma((CHUNKS,)),
            dma((7,)),
            dma((CHUNKS + 4,)),
        ],
        compiler_params=pltpu.CompilerParams(
            collective_id=0, has_side_effects=True, vmem_limit_bytes=VMEM_BYTES
        ),
    )(owners.reshape(1, blocks), gradients, left_roots, right_roots, left_stats, right_stats)
    parts = sum(out.shape[0] for out in outs)
    return pl.pallas_call(
        functools.partial(hand_over, len(outs)),
        name="hand_over",
        out_shape=outs,
        in_specs=[hbm] * 3,
        out_specs=(hbm,) * 3,
        scratch_shapes=[pltpu.VMEM(out.shape, out.dtype) for out in outs]
        + [dma((parts,)), dma((parts,))],
        compiler_params=pltpu.CompilerParams(vmem_limit_bytes=VMEM_BYTES),
    )(*results)


def solution(mesh):
    in_specs = (
        P(None, "tensor", "dp", None),
        P("tensor"),
        P(("dp", "tensor"), None, None),
        P(("dp", "tensor"), None, None),
        P(("dp", "tensor"), None, None),
        P(("dp", "tensor"), None, None),
    )
    out_specs = (
        P(None, "tensor", "dp", None),
        P(("dp", "tensor"), None, None),
        P(("dp", "tensor"), None, None),
    )
    return jax.shard_map(
        shards_step, mesh=mesh, in_specs=in_specs, out_specs=out_specs, check_vma=False
    )
```
